32 devices in a mesh: dp: 8 (over y, x, core), tensor: 4 (over z).
Axes of the slice: x: 2, y: 2, z: 4, core: 2. Of those that a mesh axis runs over, the one named last changes fastest.
Arguments:
- tokens: bfloat16 [8192, 1024], P(('dp', 'tensor')), may hold values from -6 to 6
- cotangent: bfloat16 [8192, 1024], P(('dp', 'tensor')), may hold values from -6 to 6
- positions: int32 [8, 1024], P('dp', 'tensor'), may hold values from 0 to 4095
- segment_ids: int32 [8, 1024], P('dp'), may hold values from 0 to 3, as said below
- spatial_flag: int32 [8, 4], P('dp'), may hold values from 0 to 1
- attn_weight: float32 [4, 1024, 1024], P(None, 'dp', 'tensor'), may hold values from -6 to 6
- attn_moments: float32 [2, 4, 1024, 1024], P(None, None, 'dp', 'tensor'), may hold values from -5 to 5, as said below
- attn_ema: float32 [4, 1024, 1024], P(None, 'dp', 'tensor'), may hold values from -6 to 6
- ffn_weight: float32 [2, 1024, 4096], P(None, 'dp', 'tensor'), may hold values from -6 to 6
- ffn_moments: float32 [2, 2, 1024, 4096], P(None, None, 'dp', 'tensor'), may hold values from -5 to 5, as said below
- ffn_ema: float32 [2, 1024, 4096], P(None, 'dp', 'tensor'), may hold values from -6 to 6
- norm_weight: float32 [4, 1024], replicated, may hold values from -0.3 to 1.5, as said below
- norm_moments: float32 [2, 4, 1024], replicated, may hold values from -5 to 5, as said below
- norm_ema: float32 [4, 1024], replicated, may hold values from -0.3 to 1.5, as said below
Outputs:
- out_tokens: bfloat16 [8192, 1024], P(('dp', 'tensor'))
- grad_tokens: bfloat16 [8192, 1024], P(('dp', 'tensor'))
- attn_grad: float32 [4, 1024, 1024], P(None, 'dp', 'tensor')
- ffn_grad: float32 [2, 1024, 4096], P(None, 'dp', 'tensor')
- norm_grad: float32 [4, 1024], replicated
- attn_new: float32 [4, 1024, 1024], P(None, 'dp', 'tensor')
- attn_mom_new: float32 [2, 4, 1024, 1024], P(None, None, 'dp', 'tensor')
- attn_ema_new: float32 [4, 1024, 1024], P(None, 'dp', 'tensor')
- ffn_new: float32 [2, 1024, 4096], P(None, 'dp', 'tensor')
- ffn_mom_new: float32 [2, 2, 1024, 4096], P(None, None, 'dp', 'tensor')
- ffn_ema_new: float32 [2, 1024, 4096], P(None, 'dp', 'tensor')
- norm_new: float32 [4, 1024], replicated
- norm_mom_new: float32 [2, 4, 1024], replicated
- norm_ema_new: float32 [4, 1024], replicated
The draws below stay inside these ranges and needn't reach their ends.
Inputs may be any that keep to these rules, and one draw needn't show every extreme that they name: `segment_ids`: items are contiguous runs of cells numbered in order from 0 within each group; every item has at least one cell. `attn_moments`: entry 0 of the first dimension is the first moment, entry 1 the second moment, which is positive. `ffn_moments`: entry 0 of the first dimension is the first moment, entry 1 the second moment, which is positive. `norm_moments`: entry 0 of the first dimension is the first moment, entry 1 the second moment, which is positive. `norm_weight`: rows 0 and 2 are gains between 0.5 and 1.5, rows 1 and 3 biases. `norm_ema`: rows 0 and 2 are gains between 0.5 and 1.5, rows 1 and 3 biases.
All inputs are finite; a program needn't handle non-finite values.
Results may differ from the reference program's by a relative error of at most 0.012.
Values may be sent and summed in bfloat16 or wider, within the bound.
A program may use at most 128 MiB of HBM per device.

```python
import jax
import jax.numpy as jnp
from jax import lax

D = 1024
HEADS = 16
HD = 64
FF = 4096
TOK_DEV = 256
SEGS = 4
STEP = 5
GROUP = 1024
GROUPS = 8
TOKENS = 8192
QBLOCK = 512


def moment_pair(key, shape):
    first_key, second_key = jax.random.split(key)
    first_mom = jnp.clip(jax.random.normal(first_key, shape, jnp.float32), -5.0, 5.0)
    second_mom = jnp.exp(jax.random.uniform(second_key, shape, jnp.float32, jnp.log(0.01), 0.0))
    return jnp.stack([first_mom, second_mom])


def norm_rows(key):
    gain_key, bias_key = jax.random.split(key)
    gains = jax.random.uniform(gain_key, (2, D), jnp.float32, 0.5, 1.5)
    biases = jax.random.uniform(bias_key, (2, D), jnp.float32, -0.3, 0.3)
    return jnp.stack([gains[0], biases[0], gains[1], biases[1]])


def draw_attn_moments(key, part):
    return moment_pair(jax.random.fold_in(key, 11), (4, D, D))


def draw_ffn_moments(key, part):
    return moment_pair(jax.random.fold_in(key, 12), (2, D, FF))


def draw_norm_moments(key, part):
    return moment_pair(jax.random.fold_in(key, 13), (4, D))


def draw_norm_weight(key, part):
    return norm_rows(jax.random.fold_in(key, 14))


def draw_norm_ema(key, part):
    return norm_rows(jax.random.fold_in(key, 15))


def draw_segment_ids(key, part):
    key = jax.random.fold_in(key, 16)
    long_key, length_key = jax.random.split(key)
    long_item = jax.random.randint(long_key, (GROUPS, 1), 0, SEGS)
    short_most = max(1, TOK_DEV // SEGS)
    short_lengths = jax.random.randint(length_key, (GROUPS, SEGS), 1, short_most + 1)
    item_ids = jnp.arange(SEGS, dtype=jnp.int32)[None, :]
    lengths = jnp.where(item_ids == long_item, 0, short_lengths)
    long_length = GROUP - jnp.sum(lengths, axis=1, keepdims=True)
    lengths = jnp.where(item_ids == long_item, long_length, lengths)
    item_ends = jnp.cumsum(lengths, axis=1)
    cells = jnp.arange(GROUP, dtype=jnp.int32)
    passed = cells[None, :, None] >= item_ends[:, None, :SEGS - 1]
    return jnp.sum(passed.astype(jnp.int32), axis=2).astype(jnp.int32)


def plant(result, key, least, largest):
    index_at = [jax.random.randint(jax.random.fold_in(key, axis), (), 0, length) for axis, length in enumerate(result.shape)]
    longest = result.shape.index(max(result.shape))
    neighbour = index_at[:longest] + [(index_at[longest] + 1) % result.shape[longest]] + index_at[longest + 1:]
    return result.at[tuple(index_at)].set(least).at[tuple(neighbour)].set(largest)


def spiked(array, stream_key, source, target, parts, factor):
    owner, partner = [(jnp.arange(array.shape[position]) // (array.shape[position] // parts)).reshape([-1 if axis == position else 1 for axis in range(array.ndim)]) for position in (source, target)]
    chosen = jax.random.permutation(stream_key, parts)[partner]
    strong = (owner == chosen) | (owner == (partner + parts // 2) % parts)
    return jnp.where(strong, factor * array, array)


def block_levels(own_key, shape, pieces, smallest, high):
    def one(dim, parts):
        heights = jax.random.uniform(jax.random.fold_in(jax.random.fold_in(own_key, 6), dim), (parts,), jnp.float32, smallest / len(pieces), high / len(pieces))
        return jnp.repeat(jnp.exp(heights), shape[dim] // parts).reshape((-1,) + (1,) * (len(shape) - dim - 1))

    factor_of = one(*pieces[0])
    for cut in pieces[1:]:
        factor_of = factor_of * one(*cut)
    return factor_of


def bell_draw(stream_key, extent, width, most, pieces=(), kind=jnp.bfloat16):
    gain = block_levels(stream_key, extent, pieces, -0.22, 0.18) if pieces else 1.0
    array = jax.random.normal(stream_key, extent, jnp.float32) * width * gain
    return jnp.minimum(jnp.maximum(array, -most), most).astype(kind)


def heavy_noise(rng, shape, spread, most, pieces, heavy, held_as=jnp.bfloat16):
    array = spread * jax.random.normal(rng, shape, jnp.float32)
    if pieces:
        array = array * block_levels(rng, shape, pieces, -0.22, 0.18)
    return jnp.clip(spiked(array, jax.random.fold_in(rng, 3), *heavy), -most, most).astype(held_as)


def setup_inputs(seed: int = 0) -> dict:
    arg_keys = jax.random.split(jax.random.key(seed), 15)
    return {
        "tokens": bell_draw(arg_keys[0], (TOKENS, D), 1.0, 6.0, ((0, 32),)),
        "cotangent": heavy_noise(arg_keys[1], (TOKENS, D), 1.0, 6.0, ((0, 32),), (0, 1, 32, 2.75)),
        "positions": plant(jax.random.randint(arg_keys[2], (GROUPS, GROUP), 0, 4096), jax.random.fold_in(arg_keys[2], 1), 0, 4095).astype(jnp.int32),
        "segment_ids": draw_segment_ids(jax.random.fold_in(arg_keys[14], 71), 0),
        "spatial_flag": plant(jax.random.randint(arg_keys[4], (GROUPS, SEGS), 0, 2), jax.random.fold_in(arg_keys[4], 1), 0, 1).astype(jnp.int32),
        "attn_weight": bell_draw(arg_keys[5], (4, D, D), 1.0, 6.0, ((1, 8), (2, 4)), jnp.float32),
        "attn_moments": draw_attn_moments(jax.random.fold_in(arg_keys[14], 71), 0),
        "attn_ema": bell_draw(arg_keys[7], (4, D, D), 1.0, 6.0, ((1, 8), (2, 4)), jnp.float32),
        "ffn_weight": bell_draw(arg_keys[8], (2, D, FF), 1.0, 6.0, ((1, 8), (2, 4)), jnp.float32),
        "ffn_moments": draw_ffn_moments(jax.random.fold_in(arg_keys[14], 71), 0),
        "ffn_ema": bell_draw(arg_keys[10], (2, D, FF), 1.0, 6.0, ((1, 8), (2, 4)), jnp.float32),
        "norm_weight": draw_norm_weight(jax.random.fold_in(arg_keys[14], 71), 0),
        "norm_moments": draw_norm_moments(jax.random.fold_in(arg_keys[14], 71), 0),
        "norm_ema": draw_norm_ema(jax.random.fold_in(arg_keys[14], 71), 0),
    }


@jax.custom_vjp
def low(v):
    return lax.optimization_barrier(v.astype(jnp.bfloat16)).astype(jnp.float32)

@jax.custom_vjp
def low_back(v):
    return v

def low_keep(v):
    return (low(v), None)

def low_pass(kept, grad):
    return (grad,)

def back_keep(v):
    return (v, None)

def back_low(kept, grad):
    return (low(grad),)
low.defvjp(low_keep, low_pass)
low_back.defvjp(back_keep, back_low)
highest = lax.Precision.HIGHEST
out_gain = 16.0
beta_one = 0.6
beta_two = 0.95
adam_eps = 1e-08
decay_rate = 0.1
learn_value = 0.25
ema_value = 0.7
norm_eps = 1e-05
masked_score = -1e+30

def sinusoid(cell_pos, model_width):
    feature = jnp.arange(model_width, dtype=jnp.int32)
    freqs = jnp.power(10000.0, -(2 * (feature // 2)).astype(jnp.float32) / model_width)
    angles = cell_pos.astype(jnp.float32)[:, None] * freqs[None, :]
    return jnp.where(feature % 2 == 0, jnp.sin(angles), jnp.cos(angles))

def layer_norm(inputs, gain_vec, bias_vec):
    row_mean = lax.optimization_barrier(jnp.mean(inputs, axis=-1, keepdims=True))
    centred = inputs - row_mean
    row_var = lax.optimization_barrier(jnp.mean(centred * centred, axis=-1, keepdims=True))
    return centred * lax.rsqrt(row_var + norm_eps) * gain_vec + bias_vec

def adam_update(weight, moments, ema_weight, gradient):
    step_num = float(STEP)
    first_mom = beta_one * moments[0] + (1.0 - beta_one) * gradient
    second_mom = beta_two * moments[1] + (1.0 - beta_two) * gradient * gradient
    fix_one = 1.0 - beta_one ** step_num
    fix_two = 1.0 - beta_two ** step_num
    update = first_mom / fix_one / (jnp.sqrt(second_mom / fix_two) + adam_eps) + decay_rate * weight
    new_weight = weight - learn_value * update
    new_ema = ema_value * ema_weight + (1.0 - ema_value) * new_weight
    return (new_weight, jnp.stack([first_mom, second_mom]), new_ema)

def split_heads(matrix):
    return matrix.reshape(GROUP, HEADS, HD).transpose(1, 0, 2)

def block_forward(x_embed, seg_ids, attn_weight, ffn_weight, norm_weight):
    scale_d = D ** (-0.5)
    scale_f = FF ** (-0.5)
    score_scale = HD ** (-0.5)
    h_one = low(layer_norm(x_embed, norm_weight[0], norm_weight[1]))
    queries = split_heads(low(low_back(jnp.dot(h_one, low(attn_weight[0]), precision=highest) * scale_d)))
    key_rows = split_heads(low(low_back(jnp.dot(h_one, low(attn_weight[1]), precision=highest) * scale_d)))
    val_rows = split_heads(low(low_back(jnp.dot(h_one, low(attn_weight[2]), precision=highest) * scale_d)))

    def attend(block_args):
        query_blk, seg_blk = block_args
        scores = low_back(jnp.einsum('hqd,hkd->hqk', query_blk, key_rows, precision=highest) * score_scale)
        allowed = (seg_blk[:, None] == seg_ids[None, :])[None]
        prob_rows = jax.nn.softmax(jnp.where(allowed, scores, masked_score), axis=-1)
        return jnp.einsum('hqk,hkd->hqd', low(prob_rows), val_rows, precision=highest)
    block_count = GROUP // QBLOCK
    query_blocks = queries.reshape(HEADS, block_count, QBLOCK, HD).transpose(1, 0, 2, 3)
    seg_blocks = seg_ids.reshape(block_count, QBLOCK)
    attended = lax.map(jax.checkpoint(attend), (query_blocks, seg_blocks))
    attended = attended.transpose(0, 2, 1, 3).reshape(GROUP, D)
    attended = low(low_back(attended))
    branch = low_back(jnp.dot(attended, low(attn_weight[3]).T, precision=highest) * (out_gain * scale_d))
    x_mid = x_embed + branch
    h_two = low(layer_norm(x_mid, norm_weight[2], norm_weight[3]))
    hidden = low_back(jnp.dot(h_two, low(ffn_weight[0]), precision=highest) * scale_d)
    activated = low(jax.nn.gelu(hidden, approximate=False))
    ffn_out = low_back(jnp.dot(activated, low(ffn_weight[1]).T, precision=highest) * scale_f)
    return x_mid + ffn_out

def reference(tokens, cotangent, positions, segment_ids, spatial_flag, attn_weight, attn_moments, attn_ema, ffn_weight, ffn_moments, ffn_ema, norm_weight, norm_moments, norm_ema):
    token_groups = tokens.astype(jnp.float32).reshape(GROUPS, GROUP, D)
    cot_groups = cotangent.astype(jnp.float32).reshape(GROUPS, GROUP, D)

    def one_group(totals, group_args):
        x_rows, dy_rows, cell_pos, seg_ids, flags = group_args
        item_ids = jnp.arange(SEGS, dtype=jnp.int32)
        cell_flag = lax.optimization_barrier(jnp.sum(jnp.where(seg_ids[:, None] == item_ids[None, :], flags[None, :], 0), axis=1))
        x_embed = x_rows + cell_flag.astype(jnp.float32)[:, None] * sinusoid(cell_pos, D)

        def forward(x_in, attn_in, ffn_in, norm_in):
            return block_forward(x_in, seg_ids, attn_in, ffn_in, norm_in)
        out_rows, pull_back = jax.vjp(forward, x_embed, attn_weight, ffn_weight, norm_weight)
        grad_x, grad_attn, grad_ffn, grad_norm = pull_back(dy_rows)
        totals = (totals[0] + grad_attn, totals[1] + grad_ffn, totals[2] + grad_norm)
        return (totals, (out_rows.astype(jnp.bfloat16), grad_x.astype(jnp.bfloat16)))
    zero_sums = (jnp.zeros((4, D, D), jnp.float32), jnp.zeros((2, D, FF), jnp.float32), jnp.zeros((4, D), jnp.float32))
    totals, (out_groups, dx_groups) = lax.scan(one_group, zero_sums, (token_groups, cot_groups, positions, segment_ids, spatial_flag))
    attn_grad, ffn_grad, norm_grad = totals
    grad_scale = float(TOKENS) ** (-0.5)
    attn_new, attn_mom_new, attn_ema_new = adam_update(attn_weight, attn_moments, attn_ema, attn_grad * grad_scale)
    ffn_new, ffn_mom_new, ffn_ema_new = adam_update(ffn_weight, ffn_moments, ffn_ema, ffn_grad * grad_scale)
    norm_new, norm_mom_new, norm_ema_new = adam_update(norm_weight, norm_moments, norm_ema, norm_grad * grad_scale)
    return (out_groups.reshape(TOKENS, D), dx_groups.reshape(TOKENS, D), attn_grad, ffn_grad, norm_grad, attn_new, attn_mom_new, attn_ema_new, ffn_new, ffn_mom_new, ffn_ema_new, norm_new, norm_mom_new, norm_ema_new)
```

```python
import jax
import jax.numpy as jnp
import numpy as np
from jax import lax
from jax.experimental import pallas as pl
from jax.experimental.pallas import tpu as pltpu
from jax.sharding import PartitionSpec as P

HD = 64
FF = 4096
STEP = 5


out_gain = 16.0
beta_one = 0.6
beta_two = 0.95
adam_eps = 1e-08
decay_rate = 0.1
learn_value = 0.25
ema_value = 0.7
norm_eps = 1e-05
masked_score = -1e30


def sinusoid(cell_pos, model_width):
    feature = jnp.arange(model_width, dtype=jnp.int32)
    freqs = jnp.power(10000.0, -(2 * (feature // 2)).astype(jnp.float32) / model_width)
    angles = cell_pos.astype(jnp.float32)[:, None] * freqs[None, :]
    return jnp.where(feature % 2 == 0, jnp.sin(angles), jnp.cos(angles))


def layer_norm(inputs, gain_vec, bias_vec):
    row_mean = jnp.mean(inputs, axis=-1, keepdims=True)
    centred = inputs - row_mean
    row_var = jnp.mean(centred * centred, axis=-1, keepdims=True)
    return centred * lax.rsqrt(row_var + norm_eps) * gain_vec + bias_vec


def exact_gelu(values):
    return jax.nn.gelu(values, approximate=False)


def adam_update(weight, moments, ema_weight, gradient):
    step_num = float(STEP)
    first_mom = beta_one * moments[0] + (1.0 - beta_one) * gradient
    second_mom = beta_two * moments[1] + (1.0 - beta_two) * gradient * gradient
    fix_one = 1.0 - beta_one**step_num
    fix_two = 1.0 - beta_two**step_num
    update = first_mom / fix_one / (jnp.sqrt(second_mom / fix_two) + adam_eps) + decay_rate * weight
    new_weight = weight - learn_value * update
    new_ema = ema_value * ema_weight + (1.0 - ema_value) * new_weight
    return (new_weight, jnp.stack([first_mom, second_mom]), new_ema)


def dot_last(left, right):
    return lax.dot_general(
        left, right, (((1,), (1,)), ((), ())), preferred_element_type=jnp.float32
    )


def dot_first(left, right):
    return lax.dot_general(
        left, right, (((0,), (0,)), ((), ())), preferred_element_type=jnp.float32
    )


def local(
    tokens,
    cotangent,
    positions,
    segment_ids,
    spatial_flag,
    attn_weight,
    attn_moments,
    attn_ema,
    ffn_weight,
    ffn_moments,
    ffn_ema,
    norm_weight,
    norm_moments,
    norm_ema,
):
    tok_rows = tokens.shape[0]
    model_width = tokens.shape[1]
    seg_all = segment_ids[0]
    group_len = seg_all.shape[0]
    q_block = min(512, group_len)
    block_count = group_len // q_block
    scale_d = model_width ** (-0.5)
    scale_f = FF ** (-0.5)
    score_scale = HD ** (-0.5)
    out_scale = out_gain * scale_d
    grad_scale = float(group_len * lax.axis_size("dp")) ** (-0.5)
    row_first = lax.axis_index("tensor") * tok_rows
    seg_own = lax.dynamic_slice_in_dim(seg_all, row_first, tok_rows, 0)
    item_ids = jnp.arange(spatial_flag.shape[1], dtype=jnp.int32)
    cell_flag = jnp.sum(
        jnp.where(seg_own[:, None] == item_ids[None, :], spatial_flag[0][None, :], 0), axis=1
    )
    x_embed = tokens.astype(jnp.float32) + cell_flag.astype(jnp.float32)[:, None] * sinusoid(
        positions[0], model_width
    )
    attn_half, ffn_half = (
        lax.all_gather(attn_weight.astype(jnp.bfloat16), "dp", axis=1, tiled=True),
        lax.all_gather(ffn_weight.astype(jnp.bfloat16), "dp", axis=1, tiled=True),
    )
    head_width = attn_half.shape[2]
    head_count = head_width // HD
    h_one_f, norm_one_pull = jax.vjp(layer_norm, x_embed, norm_weight[0], norm_weight[1])
    h_one = lax.all_gather(h_one_f.astype(jnp.bfloat16), "tensor", axis=0, tiled=True)
    projected = (
        jnp.einsum("gd,cdj->cgj", h_one, attn_half[:3], preferred_element_type=jnp.float32)
        * scale_d
    ).astype(jnp.bfloat16)
    queries = projected[0].reshape(group_len, head_count, HD)
    key_rows = projected[1].reshape(group_len, head_count, HD)
    val_rows = projected[2].reshape(group_len, head_count, HD)

    def score_block(block_index):
        row_start = block_index * q_block
        query_blk = lax.dynamic_slice_in_dim(queries, row_start, q_block, 0)
        seg_blk = lax.dynamic_slice_in_dim(seg_all, row_start, q_block, 0)
        scores = (
            jnp.einsum("qhd,khd->hqk", query_blk, key_rows, preferred_element_type=jnp.float32)
            * score_scale
        )
        allowed = (seg_blk[:, None] == seg_all[None, :])[None]
        return (query_blk, jnp.where(allowed, scores, masked_score), allowed)

    def attend(block_index):
        query_blk, scores, allowed = score_block(block_index)
        row_top = jnp.max(scores, axis=2, keepdims=True)
        exp_rows = jnp.exp(scores - row_top)
        row_total = jnp.sum(exp_rows, axis=2, keepdims=True)
        prob_rows = (exp_rows / row_total).astype(jnp.bfloat16)
        result = jnp.einsum("hqk,khd->qhd", prob_rows, val_rows, preferred_element_type=jnp.float32)
        return (result, (row_top + jnp.log(row_total))[:, :, 0])

    attended, log_totals = lax.map(attend, jnp.arange(block_count))
    attended = attended.reshape(group_len, head_width).astype(jnp.bfloat16)
    branch = lax.psum_scatter(
        dot_last(attended, attn_half[3]) * out_scale, "tensor", scatter_dimension=0, tiled=True
    )
    x_mid = x_embed + branch
    h_two_f, norm_two_pull = jax.vjp(layer_norm, x_mid, norm_weight[2], norm_weight[3])
    h_two = lax.all_gather(h_two_f.astype(jnp.bfloat16), "tensor", axis=0, tiled=True)
    hidden = jnp.dot(h_two, ffn_half[0], preferred_element_type=jnp.float32) * scale_d
    activated_f, gelu_pull = jax.vjp(exact_gelu, hidden)
    activated = activated_f.astype(jnp.bfloat16)
    ffn_out = lax.psum_scatter(
        dot_last(activated, ffn_half[1]) * scale_f, "tensor", scatter_dimension=0, tiled=True
    )
    out_tokens = (x_mid + ffn_out).astype(jnp.bfloat16)
    dy_own = cotangent.astype(jnp.float32)
    dy_all = lax.all_gather(cotangent, "tensor", axis=0, tiled=True)
    d_act = jnp.dot(dy_all, ffn_half[1], preferred_element_type=jnp.float32) * scale_f
    d_hidden = gelu_pull(d_act)[0].astype(jnp.bfloat16)
    grad_down = dot_first(dy_all, activated) * scale_f
    grad_up = dot_first(h_two, d_hidden) * scale_d
    d_h_two = lax.psum_scatter(
        dot_last(d_hidden, ffn_half[0]) * scale_d, "tensor", scatter_dimension=0, tiled=True
    )
    d_mid_part, d_gain_two, d_bias_two = norm_two_pull(d_h_two)
    d_mid = dy_own + d_mid_part
    d_mid_all = lax.all_gather(d_mid.astype(jnp.bfloat16), "tensor", axis=0, tiled=True)
    d_att = (
        jnp.dot(d_mid_all, attn_half[3], preferred_element_type=jnp.float32) * out_scale
    ).astype(jnp.bfloat16)
    grad_mix = dot_first(d_mid_all, attended) * out_scale
    d_att3 = d_att.reshape(group_len, head_count, HD)

    def attend_back(state_pair, block_index):
        dk_sum, dv_sum = state_pair
        query_blk, scores, allowed = score_block(block_index)
        row_start = block_index * q_block
        dout_blk = lax.dynamic_slice_in_dim(d_att3, row_start, q_block, 0)
        prob_rows = jnp.where(allowed, jnp.exp(scores - log_totals[block_index][:, :, None]), 0.0)
        dv_sum = dv_sum + jnp.einsum(
            "hqk,qhd->khd",
            prob_rows.astype(jnp.bfloat16),
            dout_blk,
            preferred_element_type=jnp.float32,
        )
        d_prob = jnp.einsum("qhd,khd->hqk", dout_blk, val_rows, preferred_element_type=jnp.float32)
        d_score = (
            prob_rows * (d_prob - jnp.sum(d_prob * prob_rows, axis=2, keepdims=True))
        ).astype(jnp.bfloat16)
        dq_blk = (
            jnp.einsum("hqk,khd->qhd", d_score, key_rows, preferred_element_type=jnp.float32)
            * score_scale
        )
        dk_sum = (
            dk_sum
            + jnp.einsum("hqk,qhd->khd", d_score, query_blk, preferred_element_type=jnp.float32)
            * score_scale
        )
        return ((dk_sum, dv_sum), dq_blk)

    zero_keys = jnp.zeros((group_len, head_count, HD), jnp.float32)
    (dk_sum, dv_sum), dq_blocks = lax.scan(
        attend_back, (zero_keys, zero_keys), jnp.arange(block_count)
    )
    d_proj = jnp.stack(
        [
            dq_blocks.reshape(group_len, head_width),
            dk_sum.reshape(group_len, head_width),
            dv_sum.reshape(group_len, head_width),
        ]
    ).astype(jnp.bfloat16)
    grad_proj = (
        jnp.einsum("gd,cgj->cdj", h_one, d_proj, preferred_element_type=jnp.float32) * scale_d
    )
    d_h_one = lax.psum_scatter(
        jnp.einsum("cgj,cdj->gd", d_proj, attn_half[:3], preferred_element_type=jnp.float32)
        * scale_d,
        "tensor",
        scatter_dimension=0,
        tiled=True,
    )
    d_embed_part, d_gain_one, d_bias_one = norm_one_pull(d_h_one)
    grad_tokens = (d_mid + d_embed_part).astype(jnp.bfloat16)
    attn_part = jnp.concatenate([grad_proj, grad_mix[None]], axis=0)
    ffn_part = jnp.stack([grad_up, grad_down])
    attn_grad, ffn_grad = (
        lax.psum_scatter(attn_part, "dp", scatter_dimension=1, tiled=True),
        lax.psum_scatter(ffn_part, "dp", scatter_dimension=1, tiled=True),
    )
    norm_grad = lax.psum(
        jnp.stack([d_gain_one, d_bias_one, d_gain_two, d_bias_two]), ("dp", "tensor")
    )
    attn_new, attn_mom_new, attn_ema_new = adam_update(
        attn_weight, attn_moments, attn_ema, attn_grad * grad_scale
    )
    ffn_new, ffn_mom_new, ffn_ema_new = adam_update(
        ffn_weight, ffn_moments, ffn_ema, ffn_grad * grad_scale
    )
    norm_new, norm_mom_new, norm_ema_new = adam_update(
        norm_weight, norm_moments, norm_ema, norm_grad * grad_scale
    )
    return (
        out_tokens,
        grad_tokens,
        attn_grad,
        ffn_grad,
        norm_grad,
        attn_new,
        attn_mom_new,
        attn_ema_new,
        ffn_new,
        ffn_mom_new,
        ffn_ema_new,
        norm_new,
        norm_mom_new,
        norm_ema_new,
    )


MESH = pl.DeviceIdType.MESH
TOK = 256
CHUNK = 32
PIECES = ("qkv", "out", "up", "down")


def contract(left, right, left_dim, right_dim):
    return lax.dot_general(
        left,
        right,
        (((left_dim,), (right_dim,)), ((), ())),
        preferred_element_type=jnp.float32,
    )


def flip(bit):
    return 1 - bit


def aligned(start, size):
    return pl.ds(pl.multiple_of(start, size), size)


def sin_cos(angle, odd):
    turns = jnp.floor(angle * (2.0 / np.pi) + 0.5)
    rest = angle - turns * 1.5703125
    rest = rest - turns * 4.837512969970703125e-4
    rest = rest - turns * 7.54978995489188216e-8
    quadrant = turns.astype(jnp.int32) + odd
    square = rest * rest
    sine = ((-1.9515295891e-4 * square + 8.3321608736e-3) * square - 1.6666654611e-1) * square
    sine = sine * rest + rest
    cosine = (2.443315711809948e-5 * square - 1.388731625493765e-3) * square
    cosine = (cosine + 4.166664568298827e-2) * square * square - 0.5 * square + 1.0
    value = jnp.where((quadrant & 1) == 1, cosine, sine)
    return jnp.where((quadrant & 2) == 2, -value, value)


def normalized(rows):
    centred = rows - jnp.mean(rows, axis=-1, keepdims=True)
    spread = lax.rsqrt(jnp.mean(centred * centred, axis=-1, keepdims=True) + norm_eps)
    return centred * spread, spread


def fold_rows(values):
    total = values[0:8]
    for first in range(8, values.shape[0], 8):
        total = total + values[first : first + 8]
    return total


def block_kernel(
    tok_in,
    cot_in,
    info_in,
    attn_in,
    ffn_in,
    norm_in,
    freq_in,
    tok_out,
    grad_out,
    attn_parts,
    ffn_parts,
    norm_out,
    info,
    tok_buf,
    g_all,
    cols,
    seg_col,
    x_embed,
    x_mid,
    d_mid,
    h_one,
    h_two,
    d_mid_all,
    attn_w,
    ffn_w,
    qkv,
    prob,
    att,
    d_att,
    act,
    d_hid,
    send_a,
    send_b,
    recv_a,
    recv_b,
    acc_a,
    acc_b,
    d_qkv,
    kv_send,
    kv_recv,
    dk_tmp,
    dv_tmp,
    ffn_sum,
    attn_stage,
    attn_sum,
    ffn_box,
    attn_box,
    norm_acc,
    norm_recv,
    one_send,
    one_recv,
    two_send,
    two_recv,
    sib_send,
    sib_recv,
    act_send,
    act_recv,
    grad_sib_send,
    grad_sib_recv,
    grad_box_send,
    grad_box_recv,
    grad_own_send,
    grad_own_recv,
    norm_send_sem,
    norm_recv_sem,
):
    width = freq_in.shape[1]
    scale_d = width ** (-0.5)
    scale_f = FF ** (-0.5)
    out_scale = out_gain * scale_d
    score_scale = HD ** (-0.5)

    d = lax.axis_index("dp")
    t = lax.axis_index("tensor")
    core = lax.rem(d, 2)
    col = lax.div(d, 2)
    x_bit = lax.rem(col, 2)
    y_bit = lax.div(col, 2)
    par = lax.rem(t, 2)
    half = lax.div(t, 2)
    quarter = 2 * par + core
    home = core == half
    d_sib = d + 1 - 2 * core
    d_x = d + 2 - 4 * x_bit
    d_y = d + 4 - 8 * y_bit
    d_xy = d_x + 4 - 8 * y_bit
    t_pair = t + 1 - 2 * par
    t_far = t + 2 - 4 * half
    sib = (d_sib, t)
    pair = (d, t_pair)
    swap = (d_sib, t_far)
    nears = ((d_x, t), (d_y, t), (d_xy, t))
    near_cols = (lax.div(d_x, 2), lax.div(d_y, 2), lax.div(d_xy, 2))

    def remote(src, dst, send, recv, device):
        return pltpu.make_async_remote_copy(
            src_ref=src, dst_ref=dst, send_sem=send, recv_sem=recv, device_id=device, device_id_type=MESH
        )

    barrier = pltpu.get_barrier_semaphore()
    peers = list(nears)
    for dd in (d, d_sib):
        for tt in (t, t_pair, t_far, t_pair + t_far - t):
            peers.append((dd, tt))
    peers = peers[:3] + peers[4:]
    for peer in peers:
        pl.semaphore_signal(barrier, inc=1, device_id=peer, device_id_type=MESH)
    pl.semaphore_wait(barrier, len(peers))

    own = aligned(par * TOK, TOK)
    other = aligned(flip(par) * TOK, TOK)

    def swap_in(src, dst, index):
        @pl.when(home)
        def _():
            pltpu.make_async_copy(src, dst, act_recv.at[index]).start()

        @pl.when(jnp.logical_not(home))
        def _():
            remote(src, dst, act_send.at[index], act_recv.at[index], swap).start()

    def swap_wait(src, dst, index):
        pltpu.make_async_copy(src, dst, act_recv.at[index]).wait()

    def swap_sent(src, dst, index):
        @pl.when(jnp.logical_not(home))
        def _():
            remote(src, dst, act_send.at[index], act_recv.at[index], swap).wait_send()

    def piece_view(piece, h, rows):
        if piece == 0:
            return attn_w.at[h, 0:3, rows, :]
        if piece == 1:
            return attn_w.at[h, 3, rows, :]
        return ffn_w.at[h, piece - 2, rows, :]

    def piece_source(piece):
        if piece == 0:
            return attn_in.at[0:3]
        if piece == 1:
            return attn_in.at[3]
        return ffn_in.at[piece - 2]

    def one_copy(piece, k):
        dst = piece_view(piece, par, aligned(d * 128, 128))
        target = (d - core + par, half + 2 * k)
        return remote(
            piece_source(piece), dst, one_send.at[piece, k], one_recv.at[piece, core], target
        )

    def one_is_own(k):
        if k == 0:
            return jnp.logical_and(core == par, t == half)
        return jnp.logical_and(core == par, t == half + 2)

    def one_start(piece):
        for k in range(2):

            @pl.when(one_is_own(k))
            def _():
                dst = piece_view(piece, par, aligned(d * 128, 128))
                pltpu.make_async_copy(piece_source(piece), dst, one_recv.at[piece, core]).start()

            @pl.when(jnp.logical_not(one_is_own(k)))
            def _():
                one_copy(piece, k).start()

    def one_sent(piece):
        for k in range(2):

            @pl.when(jnp.logical_not(one_is_own(k)))
            def _():
                one_copy(piece, k).wait_send()

    def two_copy(piece, k):
        view = piece_view(piece, core, aligned(col * 256, 256))
        return remote(view, view, two_send.at[piece, k], two_recv.at[piece, k], nears[k])

    def sib_copy(piece, k):
        which = col if k == 0 else near_cols[k - 1]
        view = piece_view(piece, core, aligned(which * 256, 256))
        return remote(view, view, sib_send.at[piece, k], sib_recv.at[piece, k], sib)

    def spread(piece):
        for c0 in range(2):
            rows = aligned((2 * col + c0) * 128, 128)
            pltpu.make_async_copy(
                piece_source(piece), piece_view(piece, core, rows), one_recv.at[piece, c0]
            ).wait()
        for k in range(3):
            two_copy(piece, k).start()
        sib_copy(piece, 0).start()

    def relay(piece):
        for k in range(3):
            two_copy(piece, k).wait_recv()
            sib_copy(piece, k + 1).start()

    def ready(piece):
        for k in range(4):
            sib_copy(piece, k).wait_recv()

    def sent(piece):
        for k in range(3):
            two_copy(piece, k).wait_send()
        for k in range(4):
            sib_copy(piece, k).wait_send()

    swap_in(info_in, info, 0)
    one_start(0)
    swap_in(tok_in, tok_buf, 1)
    swap_wait(info_in, info, 0)

    seg_first = (2 * core + par) * TOK
    seg_mine = info[0:1, aligned(seg_first, TOK)]
    flags = jnp.zeros_like(seg_mine)
    for item in range(4):
        flags = flags + jnp.where(seg_mine == item, info[2:3, item : item + 1], 0)

    def as_column(row):
        row = row.astype(jnp.float32)
        return jnp.transpose(jnp.broadcast_to(row, (128, row.shape[1])))

    cols[0] = as_column(info[1:2, 0:TOK])
    cols[1] = as_column(flags)
    seg_col[...] = as_column(info[0:1, aligned(core * 512, 512)])
    seg_row = info[0:1, :].astype(jnp.float32)
    odd = lax.rem(lax.broadcasted_iota(jnp.int32, (1, width), 1), 2)

    def encode(step, carry):
        rows = aligned(step * CHUNK, CHUNK)
        angle = cols[0, rows, 0:1] * freq_in[0:1, :]
        x_embed[rows, :] = cols[1, rows, 0:1] * sin_cos(angle, odd)
        return carry

    lax.fori_loop(0, TOK // CHUNK, encode, 0)

    spread(0)
    one_start(1)
    swap_in(cot_in, g_all.at[own, :], 2)
    one_start(2)
    one_start(3)
    swap_wait(tok_in, tok_buf, 1)

    def norm_first(step, carry):
        rows = aligned(step * CHUNK, CHUNK)
        value = x_embed[rows, :] + tok_buf[rows, :].astype(jnp.float32)
        x_embed[rows, :] = value
        unit, _ = normalized(value)
        row = aligned(par * TOK + step * CHUNK, CHUNK)
        h_one[row, :] = (unit * norm_in[0:1, :] + norm_in[1:2, :]).astype(jnp.bfloat16)
        return carry

    lax.fori_loop(0, TOK // CHUNK, norm_first, 0)

    def pair_copy(buf, index):
        return remote(buf.at[own, :], buf.at[own, :], act_send.at[index], act_recv.at[index], pair)

    pair_copy(h_one, 3).start()
    relay(0)
    spread(1)
    ready(0)
    swap_wait(cot_in, g_all.at[own, :], 2)
    pair_copy(g_all, 4).start()
    spread(2)

    def project(first):
        rows = aligned(first * TOK, TOK)
        where = aligned(core * 512 + first * TOK, TOK)

        def step(i, carry):
            h = lax.div(i, 3)
            m = lax.rem(i, 3)
            out = contract(h_one[rows, :], attn_w[h, m], 1, 0) * scale_d
            qkv[m, h, where, :] = out.astype(jnp.bfloat16)
            return carry

        lax.fori_loop(0, 6, step, 0)

    def kv_copy(first, index):
        view = qkv.at[1:3, :, aligned(core * 512 + first * TOK, TOK), :]
        return remote(view, view, act_send.at[index], act_recv.at[index], sib)

    project(par)
    kv_copy(par, 5).start()
    pair_copy(h_one, 3).wait_recv()
    project(flip(par))
    kv_copy(flip(par), 6).start()
    relay(1)
    spread(3)
    kv_copy(par, 5).wait_recv()
    kv_copy(flip(par), 6).wait_recv()

    lane_half = lax.broadcasted_iota(jnp.int32, (TOK, 128), 1)
    lane_masks = (lane_half < HD, lane_half >= HD)

    def attend(i, carry):
        jj = lax.div(i, 2)
        rows = aligned(lax.rem(i, 2) * TOK, TOK)
        q_rows = aligned(core * 512 + lax.rem(i, 2) * TOK, TOK)
        h = lax.div(jj, 2)
        lanes = aligned(lax.rem(jj, 2) * 128, 128)
        queries = qkv[0, h, q_rows, lanes] * jnp.bfloat16(score_scale)
        keys = qkv[1, h, :, lanes]
        vals = qkv[2, h, :, lanes]
        allowed = seg_col[rows, 0:1] == seg_row
        outs = []
        for a in range(2):
            query = jnp.where(lane_masks[a], queries, jnp.bfloat16(0))
            scores = jnp.where(allowed, contract(query, keys, 1, 1), masked_score)
            top = jnp.max(scores, axis=1, keepdims=True)
            weight = jnp.exp(scores - top)
            total = jnp.sum(weight, axis=1, keepdims=True)
            share = (weight * (1.0 / total)).astype(jnp.bfloat16)
            prob[2 * jj + a, rows, :] = share
            outs.append(contract(share, vals, 1, 0))
        att[h, rows, lanes] = jnp.where(lane_masks[0], outs[0], outs[1]).astype(jnp.bfloat16)
        return carry

    lax.fori_loop(0, 8, attend, 0)

    ready(1)
    relay(2)

    def split_product(product, scale, send_buf, recv_buf, acc, index, steps):
        def step_send(n, carry):
            lanes = aligned(n * TOK, TOK)
            send_buf[:, lanes] = (product(other, n) * scale).astype(jnp.bfloat16)
            return carry

        lax.fori_loop(0, steps, step_send, 0)
        remote(send_buf, recv_buf, act_send.at[index], act_recv.at[index], pair).start()

        def step_keep(n, carry):
            lanes = aligned(n * TOK, TOK)
            acc[:, lanes] = product(own, n) * scale
            return carry

        lax.fori_loop(0, steps, step_keep, 0)

    def split_wait(send_buf, recv_buf, index):
        remote(send_buf, recv_buf, act_send.at[index], act_recv.at[index], pair).wait()

    def out_product(rows, n):
        outs = aligned(n * TOK, TOK)
        total = contract(att[0, rows, :], attn_w[0, 3, outs, :], 1, 1)
        return total + contract(att[1, rows, :], attn_w[1, 3, outs, :], 1, 1)

    split_product(out_product, out_scale, send_a, recv_a, acc_a, 7, 4)
    relay(3)
    split_wait(send_a, recv_a, 7)

    def norm_second(step, carry):
        rows = aligned(step * CHUNK, CHUNK)
        value = x_embed[rows, :] + (acc_a[rows, :] + recv_a[rows, :].astype(jnp.float32))
        x_mid[rows, :] = value
        unit, _ = normalized(value)
        row = aligned(par * TOK + step * CHUNK, CHUNK)
        h_two[row, :] = (unit * norm_in[2:3, :] + norm_in[3:4, :]).astype(jnp.bfloat16)
        return carry

    lax.fori_loop(0, TOK // CHUNK, norm_second, 0)
    pair_copy(h_two, 8).start()
    pair_copy(g_all, 4).wait_recv()
    ready(2)
    ready(3)

    def feed(first):
        rows = aligned(first * TOK, TOK)

        def step(i, carry):
            h = lax.div(i, 4)
            lanes = aligned(lax.rem(i, 4) * 256, 256)
            hidden = contract(h_two[rows, :], ffn_w[h, 0, :, lanes], 1, 0) * scale_d
            d_act = contract(g_all[rows, :], ffn_w[h, 1, :, lanes], 1, 0) * scale_f
            gate = 0.5 + 0.5 * lax.erf(hidden * np.float32(np.sqrt(0.5)))
            act[h, rows, lanes] = (hidden * gate).astype(jnp.bfloat16)
            bell = jnp.exp(-0.5 * hidden * hidden) * np.float32(1.0 / np.sqrt(2.0 * np.pi))
            d_hid[h, rows, lanes] = (d_act * (gate + hidden * bell)).astype(jnp.bfloat16)
            return carry

        lax.fori_loop(0, 8, step, 0)

    feed(par)
    pair_copy(h_two, 8).wait_recv()
    feed(flip(par))

    def hid_product(rows, n):
        outs = aligned(n * TOK, TOK)
        total = contract(d_hid[0, rows, :], ffn_w[0, 0, outs, :], 1, 1)
        return total + contract(d_hid[1, rows, :], ffn_w[1, 0, outs, :], 1, 1)

    split_product(hid_product, scale_d, send_a, recv_a, acc_a, 9, 4)

    def down_product(rows, n):
        outs = aligned(n * TOK, TOK)
        total = contract(act[0, rows, :], ffn_w[0, 1, outs, :], 1, 1)
        return total + contract(act[1, rows, :], ffn_w[1, 1, outs, :], 1, 1)

    split_product(down_product, scale_f, send_b, recv_b, acc_b, 10, 4)
    for piece in range(4):
        one_sent(piece)
        sent(piece)

    def grad_tile(kind, m, h, tile):
        cells = aligned(tile * 256, 256)
        if kind == 0:
            left = h_one[:, cells] if m < 3 else d_mid_all[:, cells]
            right = d_qkv[m, h] if m < 3 else att[h]
            return contract(left, right, 0, 0) * (scale_d if m < 3 else out_scale)
        left = h_two[:, cells] if m == 0 else g_all[:, cells]
        right = d_hid[h] if m == 0 else act[h]
        return contract(left, right, 0, 0) * (scale_d if m == 0 else scale_f)

    def stage_view(kind, m, rows):
        return attn_stage.at[m, rows, :] if kind == 0 else ffn_w.at[0, m, rows, :]

    def sum_view(kind, m, rows):
        return attn_sum.at[m, rows, :] if kind == 0 else ffn_sum.at[m, rows, :]

    def slot(kind, m):
        return m if kind == 0 else 4 + m

    def tile_copy(kind, m, tile):
        rows = aligned(tile * 256, 256)
        index = slot(kind, m)
        return remote(
            stage_view(kind, m, rows),
            sum_view(kind, m, rows),
            grad_sib_send.at[index, tile],
            grad_sib_recv.at[index, tile],
            sib,
        )

    def grads_sibling(kind, m):
        def step(tile, carry):
            rows = aligned(tile * 256, 256)
            stage = stage_view(kind, m, rows)
            stage[...] = grad_tile(kind, m, flip(core), tile).astype(jnp.bfloat16)
            tile_copy(kind, m, tile).start()
            return carry

        lax.fori_loop(0, 4, step, 0)

    def tile_place(k):
        to_x = 1 - lax.div(k, 2)
        to_y = 1 - lax.rem(k, 2)
        x_new = x_bit + to_x - 2 * x_bit * to_x
        y_new = y_bit + to_y - 2 * y_bit * to_y
        return 2 * y_new + x_new

    def box_view(kind, m, k):
        return attn_box.at[k, m] if kind == 0 else ffn_box.at[k, m]

    def box_copy(kind, m, k):
        place = tile_place(k)
        index = slot(kind, m)
        return remote(
            sum_view(kind, m, aligned(place * 256, 256)),
            box_view(kind, m, k),
            grad_box_send.at[index, k],
            grad_box_recv.at[index, k],
            (2 * place + core, t),
        )

    def grads_own(kind, m):
        def step(k, carry):
            place = tile_place(k)
            total = grad_tile(kind, m, core, place)
            tile_copy(kind, m, place).wait_recv()
            view = sum_view(kind, m, aligned(place * 256, 256))
            view[...] = (total + view[...].astype(jnp.float32)).astype(jnp.bfloat16)

            @pl.when(k < 3)
            def _():
                box_copy(kind, m, k).start()

            return carry

        lax.fori_loop(0, 4, step, 0)

    def own_copy(kind, m, c0):
        rows = aligned(col * 256 + c0 * 128, 128)
        dst = attn_parts.at[half, m] if kind == 0 else ffn_parts.at[half, m]
        index = slot(kind, m)
        return remote(
            sum_view(kind, m, rows),
            dst,
            grad_own_send.at[index, c0],
            grad_own_recv.at[index, half],
            (d - core + c0, quarter),
        )

    def own_is_here(c0):
        return jnp.logical_and(core == c0, t == quarter)

    def grads_columns(kind, m):
        for k in range(3):
            box_copy(kind, m, k).wait_recv()

        def step(i, carry):
            rows = aligned(col * 256 + i * CHUNK, CHUNK)
            part = aligned(i * CHUNK, CHUNK)
            view = sum_view(kind, m, rows)
            total = view[...].astype(jnp.float32)
            for k in range(3):
                total = total + box_view(kind, m, k)[part, :].astype(jnp.float32)
            view[...] = total.astype(jnp.bfloat16)
            return carry

        lax.fori_loop(0, 256 // CHUNK, step, 0)
        for c0 in range(2):

            @pl.when(own_is_here(c0))
            def _():
                rows = aligned(col * 256 + c0 * 128, 128)
                dst = attn_parts.at[half, m] if kind == 0 else ffn_parts.at[half, m]
                pltpu.make_async_copy(
                    sum_view(kind, m, rows), dst, grad_own_recv.at[slot(kind, m), half]
                ).start()

            @pl.when(jnp.logical_not(own_is_here(c0)))
            def _():
                own_copy(kind, m, c0).start()

    def grads_finish(kind, m):
        index = slot(kind, m)
        for k in range(2):
            src = sum_view(kind, m, aligned(col * 256, 128))
            dst = attn_parts.at[k, m] if kind == 0 else ffn_parts.at[k, m]
            pltpu.make_async_copy(src, dst, grad_own_recv.at[index, k]).wait()
        for k in range(4):
            tile_copy(kind, m, k).wait_send()
        for k in range(3):
            box_copy(kind, m, k).wait_send()
        for c0 in range(2):

            @pl.when(jnp.logical_not(own_is_here(c0)))
            def _():
                own_copy(kind, m, c0).wait_send()

    grads_sibling(1, 0)
    grads_sibling(1, 1)

    split_wait(send_a, recv_a, 9)

    def back_norm(step, base, gain, add, acc, out):
        rows = aligned(step * CHUNK, CHUNK)
        unit, spread_row = normalized(base[rows, :])
        d_rows = acc[rows, :] + recv_a[rows, :].astype(jnp.float32)
        scaled = d_rows * gain
        inner = jnp.mean(scaled * unit, axis=-1, keepdims=True)
        result = add + spread_row * (scaled - jnp.mean(scaled, axis=-1, keepdims=True) - unit * inner)
        out(rows, result)
        return fold_rows(d_rows * unit), fold_rows(d_rows)

    def back_second(step, carry):
        def out(rows, result):
            d_mid[rows, :] = result
            row = aligned(par * TOK + step * CHUNK, CHUNK)
            d_mid_all[row, :] = result.astype(jnp.bfloat16)

        row = aligned(par * TOK + step * CHUNK, CHUNK)
        add = g_all[row, :].astype(jnp.float32)
        d_gain, d_bias = back_norm(step, x_mid, norm_in[2:3, :], add, acc_a, out)
        norm_acc[2] = norm_acc[2] + d_gain
        norm_acc[3] = norm_acc[3] + d_bias
        return carry

    norm_acc[...] = jnp.zeros_like(norm_acc)
    lax.fori_loop(0, TOK // CHUNK, back_second, 0)
    pair_copy(d_mid_all, 11).start()

    grads_own(1, 0)
    grads_own(1, 1)

    split_wait(send_b, recv_b, 10)

    def finish_out(step, carry):
        rows = aligned(step * CHUNK, CHUNK)
        total = x_mid[rows, :] + (acc_b[rows, :] + recv_b[rows, :].astype(jnp.float32))
        tok_buf[rows, :] = total.astype(jnp.bfloat16)
        return carry

    lax.fori_loop(0, TOK // CHUNK, finish_out, 0)
    swap_in(tok_buf, tok_out, 12)

    def back_out(first):
        rows = aligned(first * TOK, TOK)

        def step(h, carry):
            out = contract(d_mid_all[rows, :], attn_w[h, 3], 1, 0) * out_scale
            d_att[h, rows, :] = out.astype(jnp.bfloat16)
            return carry

        lax.fori_loop(0, 2, step, 0)

    back_out(par)
    pair_copy(d_mid_all, 11).wait_recv()
    back_out(flip(par))
    grads_sibling(0, 3)

    def attend_back(jj, carry):
        h = lax.div(jj, 2)
        lanes = aligned(lax.rem(jj, 2) * 128, 128)
        keys = qkv[1, h, :, lanes]
        vals = qkv[2, h, :, lanes]
        dk_total = None
        dv_total = None
        for part in range(2):
            rows = pl.ds(part * TOK, TOK)
            q_rows = aligned(core * 512 + part * TOK, TOK)
            queries = qkv[0, h, q_rows, lanes] * jnp.bfloat16(score_scale)
            d_outs = d_att[h, rows, lanes]
            inner = d_outs.astype(jnp.float32) * att[h, rows, lanes].astype(jnp.float32)
            dqs = []
            for a in range(2):
                share = prob[2 * jj + a, rows, :]
                d_out = jnp.where(lane_masks[a], d_outs, jnp.bfloat16(0))
                query = jnp.where(lane_masks[a], queries, jnp.bfloat16(0))
                row_sum = jnp.sum(jnp.where(lane_masks[a], inner, 0.0), axis=1, keepdims=True)
                d_prob = contract(d_out, vals, 1, 1)
                d_score = (share.astype(jnp.float32) * (d_prob - row_sum)).astype(jnp.bfloat16)
                dqs.append(contract(d_score, keys, 1, 0))
                dk = contract(query, d_score, 0, 0)
                dv = contract(d_out, share, 0, 0)
                dk_total = dk if dk_total is None else dk_total + dk
                dv_total = dv if dv_total is None else dv_total + dv
            d_query = jnp.where(lane_masks[0], dqs[0], dqs[1]) * score_scale
            d_qkv[0, h, rows, lanes] = d_query.astype(jnp.bfloat16)
        dk_tmp[...] = dk_total
        dv_tmp[...] = dv_total
        mine = aligned(core * 512, 512)
        theirs = aligned(flip(core) * 512, 512)
        d_qkv[1, h, :, lanes] = jnp.transpose(dk_tmp[:, mine]).astype(jnp.bfloat16)
        d_qkv[2, h, :, lanes] = jnp.transpose(dv_tmp[:, mine]).astype(jnp.bfloat16)
        kv_send[jj, 0] = jnp.transpose(dk_tmp[:, theirs]).astype(jnp.bfloat16)
        kv_send[jj, 1] = jnp.transpose(dv_tmp[:, theirs]).astype(jnp.bfloat16)
        kv_grad_copy(jj).start()
        return carry

    def kv_grad_copy(jj):
        return remote(kv_send.at[jj], kv_recv.at[jj], act_send.at[13 + jj], act_recv.at[13 + jj], sib)

    lax.fori_loop(0, 4, attend_back, 0)

    def join_kv(jj, carry):
        kv_grad_copy(jj).wait()
        h = lax.div(jj, 2)
        lanes = aligned(lax.rem(jj, 2) * 128, 128)
        for m in range(2):
            total = d_qkv[m + 1, h, :, lanes].astype(jnp.float32) + kv_recv[jj, m].astype(jnp.float32)
            d_qkv[m + 1, h, :, lanes] = total.astype(jnp.bfloat16)
        return carry

    grads_columns(1, 0)
    grads_columns(1, 1)
    lax.fori_loop(0, 4, join_kv, 0)

    def first_product(rows, n):
        outs = aligned(n * TOK, TOK)
        total = None
        for h in range(2):
            for m in range(3):
                part = contract(d_qkv[m, h, rows, :], attn_w[h, m, outs, :], 1, 1)
                total = part if total is None else total + part
        return total

    split_product(first_product, scale_d, send_a, recv_a, acc_a, 17, 4)
    for m in range(3):
        grads_sibling(0, m)
    grads_own(0, 3)
    for m in range(3):
        grads_own(0, m)

    split_wait(send_a, recv_a, 17)
    swap_sent(tok_buf, tok_out, 12)
    swap_wait(tok_buf, tok_out, 12)

    def back_first(step, carry):
        def out(rows, result):
            tok_buf[rows, :] = result.astype(jnp.bfloat16)

        add = d_mid[aligned(step * CHUNK, CHUNK), :]
        d_gain, d_bias = back_norm(step, x_embed, norm_in[0:1, :], add, acc_a, out)
        norm_acc[0] = norm_acc[0] + d_gain
        norm_acc[1] = norm_acc[1] + d_bias
        return carry

    lax.fori_loop(0, TOK // CHUNK, back_first, 0)
    swap_in(tok_buf, grad_out, 18)

    for row in range(4):
        norm_out[row : row + 1, :] = jnp.sum(norm_acc[row], axis=0, keepdims=True)
    norm_out[4:8, :] = jnp.zeros((4, width), jnp.float32)
    for i, peer in enumerate((sib, nears[0], nears[1], pair, (d, t_far))):
        copy = remote(norm_out, norm_recv.at[i], norm_send_sem.at[i], norm_recv_sem.at[i], peer)
        copy.start()
        copy.wait()
        norm_out[...] = norm_out[...] + norm_recv[i]

    for m in (3, 0, 1, 2):
        grads_columns(0, m)
    for m in range(2):
        grads_finish(1, m)
    for m in range(4):
        grads_finish(0, m)
    swap_sent(tok_buf, grad_out, 18)
    swap_wait(tok_buf, grad_out, 18)
    swap_sent(info_in, info, 0)
    swap_sent(tok_in, tok_buf, 1)
    swap_sent(cot_in, g_all.at[own, :], 2)
    pair_copy(h_one, 3).wait_send()
    pair_copy(g_all, 4).wait_send()
    pair_copy(h_two, 8).wait_send()
    pair_copy(d_mid_all, 11).wait_send()
    kv_copy(par, 5).wait_send()
    kv_copy(flip(par), 6).wait_send()


def run_block(tok, cot, info, attn_half, ffn_half, norm_weight, freqs):
    bf16, f32 = jnp.bfloat16, jnp.float32
    vmem, sem = pltpu.VMEM, pltpu.SemaphoreType.DMA
    width = tok.shape[1]
    wide, ff_q, head_q = 2 * TOK, ffn_half.shape[2], attn_half.shape[2]
    group = info.shape[1]
    hbm = pl.BlockSpec(memory_space=pl.ANY)
    on_chip = pl.BlockSpec(memory_space=pltpu.VMEM)
    return pl.pallas_call(
        block_kernel,
        out_shape=(
            jax.ShapeDtypeStruct(tok.shape, bf16),
            jax.ShapeDtypeStruct(tok.shape, bf16),
            jax.ShapeDtypeStruct((2,) + attn_half.shape, bf16),
            jax.ShapeDtypeStruct((2,) + ffn_half.shape, bf16),
            jax.ShapeDtypeStruct((8, width), f32),
        ),
        in_specs=[hbm, hbm, hbm, hbm, hbm, on_chip, on_chip],
        out_specs=(hbm, hbm, hbm, hbm, on_chip),
        scratch_shapes=[
            vmem((8, group), jnp.int32),
            vmem((TOK, width), bf16),
            vmem((wide, width), bf16),
            vmem((2, TOK, 128), f32),
            vmem((wide, 128), f32),
            vmem((TOK, width), f32),
            vmem((TOK, width), f32),
            vmem((TOK, width), f32),
            vmem((wide, width), bf16),
            vmem((wide, width), bf16),
            vmem((wide, width), bf16),
            vmem((2, 4, width, head_q), bf16),
            vmem((2, 2, width, ff_q), bf16),
            vmem((3, 2, group, head_q), bf16),
            vmem((8, wide, group), bf16),
            vmem((2, wide, head_q), bf16),
            vmem((2, wide, head_q), bf16),
            vmem((2, wide, ff_q), bf16),
            vmem((2, wide, ff_q), bf16),
            vmem((TOK, width), bf16),
            vmem((TOK, width), bf16),
            vmem((TOK, width), bf16),
            vmem((TOK, width), bf16),
            vmem((TOK, width), f32),
            vmem((TOK, width), f32),
            vmem((3, 2, wide, head_q), bf16),
            vmem((4, 2, wide, 128), bf16),
            vmem((4, 2, wide, 128), bf16),
            vmem((128, group), f32),
            vmem((128, group), f32),
            vmem((2, width, ff_q), bf16),
            vmem((4, width, head_q), bf16),
            vmem((4, width, head_q), bf16),
            vmem((3, 2, 256, ff_q), bf16),
            vmem((3, 4, 256, head_q), bf16),
            vmem((4, 8, width), f32),
            vmem((5, 8, width), f32),
            sem((4, 2)),
            sem((4, 2)),
            sem((4, 3)),
            sem((4, 3)),
            sem((4, 4)),
            sem((4, 4)),
            sem((19,)),
            sem((19,)),
            sem((6, 4)),
            sem((6, 4)),
            sem((6, 3)),
            sem((6, 3)),
            sem((6, 2)),
            sem((6, 2)),
            sem((5,)),
            sem((5,)),
        ],
        compiler_params=pltpu.CompilerParams(
            collective_id=0, has_side_effects=True, vmem_limit_bytes=VMEM_LIMIT
        ),
        cost_estimate=pl.CostEstimate(
            flops=30_000_000_000, bytes_accessed=30_000_000, transcendentals=10_000_000
        ),
        name="block",
    )(tok, cot, info, attn_half, ffn_half, norm_weight, freqs)


VMEM_LIMIT = 63 * 2**20


def local_fast(
    tokens,
    cotangent,
    positions,
    segment_ids,
    spatial_flag,
    attn_weight,
    attn_moments,
    attn_ema,
    ffn_weight,
    ffn_moments,
    ffn_ema,
    norm_weight,
    norm_moments,
    norm_ema,
):
    width = tokens.shape[1]
    group = segment_ids.shape[1]
    exponent = -2.0 * (np.arange(width) // 2) / width
    freqs = jnp.asarray(np.tile((10000.0**exponent).astype(np.float32), (8, 1)))
    info = jnp.zeros((8, group), jnp.int32)
    info = info.at[0].set(segment_ids[0])
    info = info.at[1, : positions.shape[1]].set(positions[0])
    info = info.at[2, : spatial_flag.shape[1]].set(spatial_flag[0])
    grad_scale = float(group * lax.axis_size("dp")) ** (-0.5)
    out_tokens, grad_tokens, attn_parts, ffn_parts, norm_rows = run_block(
        tokens,
        cotangent,
        info,
        attn_weight.astype(jnp.bfloat16),
        ffn_weight.astype(jnp.bfloat16),
        norm_weight,
        freqs,
    )
    attn_grad = attn_parts[0].astype(jnp.float32) + attn_parts[1].astype(jnp.float32)
    ffn_grad = ffn_parts[0].astype(jnp.float32) + ffn_parts[1].astype(jnp.float32)
    norm_grad = norm_rows[:4]
    attn_new, attn_mom_new, attn_ema_new = adam_update(
        attn_weight, attn_moments, attn_ema, attn_grad * grad_scale
    )
    ffn_new, ffn_mom_new, ffn_ema_new = adam_update(
        ffn_weight, ffn_moments, ffn_ema, ffn_grad * grad_scale
    )
    norm_new, norm_mom_new, norm_ema_new = adam_update(
        norm_weight, norm_moments, norm_ema, norm_grad * grad_scale
    )
    return (
        out_tokens,
        grad_tokens,
        attn_grad,
        ffn_grad,
        norm_grad,
        attn_new,
        attn_mom_new,
        attn_ema_new,
        ffn_new,
        ffn_mom_new,
        ffn_ema_new,
        norm_new,
        norm_mom_new,
        norm_ema_new,
    )


def solution(mesh):
    placed = (
        P(("dp", "tensor"), None),
        P(("dp", "tensor"), None),
        P("dp", "tensor"),
        P("dp", None),
        P("dp", None),
        P(None, "dp", "tensor"),
        P(None, None, "dp", "tensor"),
        P(None, "dp", "tensor"),
        P(None, "dp", "tensor"),
        P(None, None, "dp", "tensor"),
        P(None, "dp", "tensor"),
        P(),
        P(),
        P(),
    )
    fast = mesh.shape["dp"] == 8 and mesh.shape["tensor"] == 4
    return jax.shard_map(
        local_fast if fast else local,
        mesh=mesh,
        in_specs=placed,
        out_specs=(
            P(("dp", "tensor"), None),
            P(("dp", "tensor"), None),
            P(None, "dp", "tensor"),
            P(None, "dp", "tensor"),
            P(),
            P(None, "dp", "tensor"),
            P(None, None, "dp", "tensor"),
            P(None, "dp", "tensor"),
            P(None, "dp", "tensor"),
            P(None, None, "dp", "tensor"),
            P(None, "dp", "tensor"),
            P(),
            P(),
            P(),
        ),
        check_vma=False,
    )
```

```python
import jax
import jax.numpy as jnp
import numpy as np
from jax import lax
from jax.experimental import pallas as pl
from jax.experimental.pallas import tpu as pltpu
from jax.sharding import PartitionSpec as P

HD = 64
FF = 4096
STEP = 5


out_gain = 16.0
beta_one = 0.6
beta_two = 0.95
adam_eps = 1e-08
decay_rate = 0.1
learn_value = 0.25
ema_value = 0.7
norm_eps = 1e-05
masked_score = -1e30


def sinusoid(cell_pos, model_width):
    feature = jnp.arange(model_width, dtype=jnp.int32)
    freqs = jnp.power(10000.0, -(2 * (feature // 2)).astype(jnp.float32) / model_width)
    angles = cell_pos.astype(jnp.float32)[:, None] * freqs[None, :]
    return jnp.where(feature % 2 == 0, jnp.sin(angles), jnp.cos(angles))


def layer_norm(inputs, gain_vec, bias_vec):
    row_mean = jnp.mean(inputs, axis=-1, keepdims=True)
    centred = inputs - row_mean
    row_var = jnp.mean(centred * centred, axis=-1, keepdims=True)
    return centred * lax.rsqrt(row_var + norm_eps) * gain_vec + bias_vec


def exact_gelu(values):
    return jax.nn.gelu(values, approximate=False)


def adam_update(weight, moments, ema_weight, gradient):
    step_num = float(STEP)
    first_mom = beta_one * moments[0] + (1.0 - beta_one) * gradient
    second_mom = beta_two * moments[1] + (1.0 - beta_two) * gradient * gradient
    fix_one = 1.0 - beta_one**step_num
    fix_two = 1.0 - beta_two**step_num
    update = first_mom / fix_one / (jnp.sqrt(second_mom / fix_two) + adam_eps) + decay_rate * weight
    new_weight = weight - learn_value * update
    new_ema = ema_value * ema_weight + (1.0 - ema_value) * new_weight
    return (new_weight, jnp.stack([first_mom, second_mom]), new_ema)


def dot_last(left, right):
    return lax.dot_general(
        left, right, (((1,), (1,)), ((), ())), preferred_element_type=jnp.float32
    )


def dot_first(left, right):
    return lax.dot_general(
        left, right, (((0,), (0,)), ((), ())), preferred_element_type=jnp.float32
    )


def local(
    tokens,
    cotangent,
    positions,
    segment_ids,
    spatial_flag,
    attn_weight,
    attn_moments,
    attn_ema,
    ffn_weight,
    ffn_moments,
    ffn_ema,
    norm_weight,
    norm_moments,
    norm_ema,
):
    tok_rows = tokens.shape[0]
    model_width = tokens.shape[1]
    seg_all = segment_ids[0]
    group_len = seg_all.shape[0]
    q_block = min(512, group_len)
    block_count = group_len // q_block
    scale_d = model_width ** (-0.5)
    scale_f = FF ** (-0.5)
    score_scale = HD ** (-0.5)
    out_scale = out_gain * scale_d
    grad_scale = float(group_len * lax.axis_size("dp")) ** (-0.5)
    row_first = lax.axis_index("tensor") * tok_rows
    seg_own = lax.dynamic_slice_in_dim(seg_all, row_first, tok_rows, 0)
    item_ids = jnp.arange(spatial_flag.shape[1], dtype=jnp.int32)
    cell_flag = jnp.sum(
        jnp.where(seg_own[:, None] == item_ids[None, :], spatial_flag[0][None, :], 0), axis=1
    )
    x_embed = tokens.astype(jnp.float32) + cell_flag.astype(jnp.float32)[:, None] * sinusoid(
        positions[0], model_width
    )
    attn_half, ffn_half = (
        lax.all_gather(attn_weight.astype(jnp.bfloat16), "dp", axis=1, tiled=True),
        lax.all_gather(ffn_weight.astype(jnp.bfloat16), "dp", axis=1, tiled=True),
    )
    head_width = attn_half.shape[2]
    head_count = head_width // HD
    h_one_f, norm_one_pull = jax.vjp(layer_norm, x_embed, norm_weight[0], norm_weight[1])
    h_one = lax.all_gather(h_one_f.astype(jnp.bfloat16), "tensor", axis=0, tiled=True)
    projected = (
        jnp.einsum("gd,cdj->cgj", h_one, attn_half[:3], preferred_element_type=jnp.float32)
        * scale_d
    ).astype(jnp.bfloat16)
    queries = projected[0].reshape(group_len, head_count, HD)
    key_rows = projected[1].reshape(group_len, head_count, HD)
    val_rows = projected[2].reshape(group_len, head_count, HD)

    def score_block(block_index):
        row_start = block_index * q_block
        query_blk = lax.dynamic_slice_in_dim(queries, row_start, q_block, 0)
        seg_blk = lax.dynamic_slice_in_dim(seg_all, row_start, q_block, 0)
        scores = (
            jnp.einsum("qhd,khd->hqk", query_blk, key_rows, preferred_element_type=jnp.float32)
            * score_scale
        )
        allowed = (seg_blk[:, None] == seg_all[None, :])[None]
        return (query_blk, jnp.where(allowed, scores, masked_score), allowed)

    def attend(block_index):
        query_blk, scores, allowed = score_block(block_index)
        row_top = jnp.max(scores, axis=2, keepdims=True)
        exp_rows = jnp.exp(scores - row_top)
        row_total = jnp.sum(exp_rows, axis=2, keepdims=True)
        prob_rows = (exp_rows / row_total).astype(jnp.bfloat16)
        result = jnp.einsum("hqk,khd->qhd", prob_rows, val_rows, preferred_element_type=jnp.float32)
        return (result, (row_top + jnp.log(row_total))[:, :, 0])

    attended, log_totals = lax.map(attend, jnp.arange(block_count))
    attended = attended.reshape(group_len, head_width).astype(jnp.bfloat16)
    branch = lax.psum_scatter(
        dot_last(attended, attn_half[3]) * out_scale, "tensor", scatter_dimension=0, tiled=True
    )
    x_mid = x_embed + branch
    h_two_f, norm_two_pull = jax.vjp(layer_norm, x_mid, norm_weight[2], norm_weight[3])
    h_two = lax.all_gather(h_two_f.astype(jnp.bfloat16), "tensor", axis=0, tiled=True)
    hidden = jnp.dot(h_two, ffn_half[0], preferred_element_type=jnp.float32) * scale_d
    activated_f, gelu_pull = jax.vjp(exact_gelu, hidden)
    activated = activated_f.astype(jnp.bfloat16)
    ffn_out = lax.psum_scatter(
        dot_last(activated, ffn_half[1]) * scale_f, "tensor", scatter_dimension=0, tiled=True
    )
    out_tokens = (x_mid + ffn_out).astype(jnp.bfloat16)
    dy_own = cotangent.astype(jnp.float32)
    dy_all = lax.all_gather(cotangent, "tensor", axis=0, tiled=True)
    d_act = jnp.dot(dy_all, ffn_half[1], preferred_element_type=jnp.float32) * scale_f
    d_hidden = gelu_pull(d_act)[0].astype(jnp.bfloat16)
    grad_down = dot_first(dy_all, activated) * scale_f
    grad_up = dot_first(h_two, d_hidden) * scale_d
    d_h_two = lax.psum_scatter(
        dot_last(d_hidden, ffn_half[0]) * scale_d, "tensor", scatter_dimension=0, tiled=True
    )
    d_mid_part, d_gain_two, d_bias_two = norm_two_pull(d_h_two)
    d_mid = dy_own + d_mid_part
    d_mid_all = lax.all_gather(d_mid.astype(jnp.bfloat16), "tensor", axis=0, tiled=True)
    d_att = (
        jnp.dot(d_mid_all, attn_half[3], preferred_element_type=jnp.float32) * out_scale
    ).astype(jnp.bfloat16)
    grad_mix = dot_first(d_mid_all, attended) * out_scale
    d_att3 = d_att.reshape(group_len, head_count, HD)

    def attend_back(state_pair, block_index):
        dk_sum, dv_sum = state_pair
        query_blk, scores, allowed = score_block(block_index)
        row_start = block_index * q_block
        dout_blk = lax.dynamic_slice_in_dim(d_att3, row_start, q_block, 0)
        prob_rows = jnp.where(allowed, jnp.exp(scores - log_totals[block_index][:, :, None]), 0.0)
        dv_sum = dv_sum + jnp.einsum(
            "hqk,qhd->khd",
            prob_rows.astype(jnp.bfloat16),
            dout_blk,
            preferred_element_type=jnp.float32,
        )
        d_prob = jnp.einsum("qhd,khd->hqk", dout_blk, val_rows, preferred_element_type=jnp.float32)
        d_score = (
            prob_rows * (d_prob - jnp.sum(d_prob * prob_rows, axis=2, keepdims=True))
        ).astype(jnp.bfloat16)
        dq_blk = (
            jnp.einsum("hqk,khd->qhd", d_score, key_rows, preferred_element_type=jnp.float32)
            * score_scale
        )
        dk_sum = (
            dk_sum
            + jnp.einsum("hqk,qhd->khd", d_score, query_blk, preferred_element_type=jnp.float32)
            * score_scale
        )
        return ((dk_sum, dv_sum), dq_blk)

    zero_keys = jnp.zeros((group_len, head_count, HD), jnp.float32)
    (dk_sum, dv_sum), dq_blocks = lax.scan(
        attend_back, (zero_keys, zero_keys), jnp.arange(block_count)
    )
    d_proj = jnp.stack(
        [
            dq_blocks.reshape(group_len, head_width),
            dk_sum.reshape(group_len, head_width),
            dv_sum.reshape(group_len, head_width),
        ]
    ).astype(jnp.bfloat16)
    grad_proj = (
        jnp.einsum("gd,cgj->cdj", h_one, d_proj, preferred_element_type=jnp.float32) * scale_d
    )
    d_h_one = lax.psum_scatter(
        jnp.einsum("cgj,cdj->gd", d_proj, attn_half[:3], preferred_element_type=jnp.float32)
        * scale_d,
        "tensor",
        scatter_dimension=0,
        tiled=True,
    )
    d_embed_part, d_gain_one, d_bias_one = norm_one_pull(d_h_one)
    grad_tokens = (d_mid + d_embed_part).astype(jnp.bfloat16)
    attn_part = jnp.concatenate([grad_proj, grad_mix[None]], axis=0)
    ffn_part = jnp.stack([grad_up, grad_down])
    attn_grad, ffn_grad = (
        lax.psum_scatter(attn_part, "dp", scatter_dimension=1, tiled=True),
        lax.psum_scatter(ffn_part, "dp", scatter_dimension=1, tiled=True),
    )
    norm_grad = lax.psum(
        jnp.stack([d_gain_one, d_bias_one, d_gain_two, d_bias_two]), ("dp", "tensor")
    )
    attn_new, attn_mom_new, attn_ema_new = adam_update(
        attn_weight, attn_moments, attn_ema, attn_grad * grad_scale
    )
    ffn_new, ffn_mom_new, ffn_ema_new = adam_update(
        ffn_weight, ffn_moments, ffn_ema, ffn_grad * grad_scale
    )
    norm_new, norm_mom_new, norm_ema_new = adam_update(
        norm_weight, norm_moments, norm_ema, norm_grad * grad_scale
    )
    return (
        out_tokens,
        grad_tokens,
        attn_grad,
        ffn_grad,
        norm_grad,
        attn_new,
        attn_mom_new,
        attn_ema_new,
        ffn_new,
        ffn_mom_new,
        ffn_ema_new,
        norm_new,
        norm_mom_new,
        norm_ema_new,
    )


MESH = pl.DeviceIdType.MESH
TOK = 256
WIDE = 512
CHUNK = 32
PIECES = ("qkv", "out", "up", "down")


def contract(left, right, left_dim, right_dim):
    return lax.dot_general(
        left,
        right,
        (((left_dim,), (right_dim,)), ((), ())),
        preferred_element_type=jnp.float32,
    )


def flip(bit):
    return 1 - bit


def aligned(start, size):
    return pl.ds(pl.multiple_of(start, size), size)


def sin_cos(angle, odd):
    turns = jnp.floor(angle * (2.0 / np.pi) + 0.5)
    rest = angle - turns * 1.5703125
    rest = rest - turns * 4.837512969970703125e-4
    rest = rest - turns * 7.54978995489188216e-8
    quadrant = turns.astype(jnp.int32) + odd
    square = rest * rest
    sine = ((-1.9515295891e-4 * square + 8.3321608736e-3) * square - 1.6666654611e-1) * square
    sine = sine * rest + rest
    cosine = (2.443315711809948e-5 * square - 1.388731625493765e-3) * square
    cosine = (cosine + 4.166664568298827e-2) * square * square - 0.5 * square + 1.0
    value = jnp.where((quadrant & 1) == 1, cosine, sine)
    return jnp.where((quadrant & 2) == 2, -value, value)


def normalized(rows):
    centred = rows - jnp.mean(rows, axis=-1, keepdims=True)
    spread = lax.rsqrt(jnp.mean(centred * centred, axis=-1, keepdims=True) + norm_eps)
    return centred * spread, spread


def fold_rows(values):
    total = values[0:8]
    for first in range(8, values.shape[0], 8):
        total = total + values[first : first + 8]
    return total


def block_kernel(
    tok_in,
    cot_in,
    pos_in,
    seg_in,
    flag_in,
    attn_in,
    ffn_in,
    norm_in,
    freq_in,
    tok_out,
    grad_out,
    attn_parts,
    ffn_parts,
    norm_out,
    info,
    tok_buf,
    g_all,
    cols,
    seg_col,
    x_embed,
    x_mid,
    d_mid,
    h_one,
    h_two,
    d_mid_all,
    attn_w,
    ffn_w,
    qkv,
    prob,
    att,
    d_att,
    act,
    d_hid,
    send_a,
    send_b,
    recv_a,
    recv_b,
    acc_a,
    acc_b,
    d_qkv,
    kv_send,
    kv_recv,
    dk_tmp,
    dv_tmp,
    ffn_sum,
    stage,
    attn_sum,
    ffn_box,
    attn_box,
    norm_acc,
    norm_recv,
    one_send,
    one_recv,
    two_send,
    two_recv,
    sib_send,
    sib_recv,
    act_send,
    act_recv,
    grad_sib_send,
    grad_sib_recv,
    grad_box_send,
    grad_box_recv,
    grad_own_send,
    grad_own_recv,
    norm_send_sem,
    norm_recv_sem,
    attn_half,
    load_sem,
    info_in,
):
    width = freq_in.shape[1]
    scale_d = width ** (-0.5)
    scale_f = FF ** (-0.5)
    out_scale = out_gain * scale_d
    score_scale = HD ** (-0.5)

    d = lax.axis_index("dp")
    t = lax.axis_index("tensor")
    core = lax.rem(d, 2)
    col = lax.div(d, 2)
    x_bit = lax.rem(col, 2)
    y_bit = lax.div(col, 2)
    par = lax.rem(t, 2)
    half = lax.div(t, 2)
    quarter = 2 * par + core
    home = core == half
    d_sib = d + 1 - 2 * core
    d_x = d + 2 - 4 * x_bit
    d_y = d + 4 - 8 * y_bit
    d_xy = d_x + 4 - 8 * y_bit
    t_pair = t + 1 - 2 * par
    t_far = t + 2 - 4 * half
    sib = (d_sib, t)
    pair = (d, t_pair)
    swap = (d_sib, t_far)
    nears = ((d_x, t), (d_y, t), (d_xy, t))
    near_cols = (lax.div(d_x, 2), lax.div(d_y, 2), lax.div(d_xy, 2))

    def remote(src, dst, send, recv, device):
        return pltpu.make_async_remote_copy(
            src_ref=src, dst_ref=dst, send_sem=send, recv_sem=recv, device_id=device, device_id_type=MESH
        )

    def load_copy(i):
        if i < 4:
            src, dst = attn_in.at[i], acc_a.at[0:128, pl.ds(i * 256, 256)]
        else:
            src, dst = ffn_in.at[i - 4], acc_b.at[pl.ds((i - 4) * 128, 128), :]
        return pltpu.make_async_copy(src, dst, load_sem.at[i])

    for i in range(6):
        load_copy(i).start()
    info_in[...] = jnp.zeros_like(info_in)
    info_in[0:1, :] = seg_in[...]
    info_in[1:2, 0:TOK] = pos_in[...]
    info_in[2:3, 0 : flag_in.shape[1]] = flag_in[...]

    barrier = pltpu.get_barrier_semaphore()
    peers = list(nears)
    for dd in (d, d_sib):
        for tt in (t, t_pair, t_far, t_pair + t_far - t):
            peers.append((dd, tt))
    peers = peers[:3] + peers[4:]
    for peer in peers:
        pl.semaphore_signal(barrier, inc=1, device_id=peer, device_id_type=MESH)
    for i in range(4):
        load_copy(i).wait()
        attn_half[i] = acc_a[0:128, i * 256 : (i + 1) * 256].astype(jnp.bfloat16)
    pl.semaphore_wait(barrier, len(peers))

    own = aligned(par * TOK, TOK)
    other = aligned(flip(par) * TOK, TOK)

    def swap_in(src, dst, index):
        @pl.when(home)
        def _():
            pltpu.make_async_copy(src, dst, act_recv.at[index]).start()

        @pl.when(jnp.logical_not(home))
        def _():
            remote(src, dst, act_send.at[index], act_recv.at[index], swap).start()

    def swap_wait(src, dst, index):
        pltpu.make_async_copy(src, dst, act_recv.at[index]).wait()

    def swap_sent(src, dst, index):
        @pl.when(jnp.logical_not(home))
        def _():
            remote(src, dst, act_send.at[index], act_recv.at[index], swap).wait_send()

    def piece_view(piece, h, rows):
        if piece == 0:
            return attn_w.at[h, 0:3, rows, :]
        if piece == 1:
            return attn_w.at[h, 3, rows, :]
        return ffn_w.at[h, piece - 2, rows, :]

    def piece_source(piece):
        if piece == 0:
            return attn_half.at[0:3]
        if piece == 1:
            return attn_half.at[3]
        return send_b.at[pl.ds((piece - 2) * 128, 128), :]

    def one_copy(piece, k):
        dst = piece_view(piece, par, aligned(d * 128, 128))
        target = (d - core + par, half + 2 * k)
        return remote(
            piece_source(piece), dst, one_send.at[piece, k], one_recv.at[piece, core], target
        )

    def one_is_own(k):
        if k == 0:
            return jnp.logical_and(core == par, t == half)
        return jnp.logical_and(core == par, t == half + 2)

    def one_start(piece):
        for k in range(2):

            @pl.when(one_is_own(k))
            def _():
                dst = piece_view(piece, par, aligned(d * 128, 128))
                pltpu.make_async_copy(piece_source(piece), dst, one_recv.at[piece, core]).start()

            @pl.when(jnp.logical_not(one_is_own(k)))
            def _():
                one_copy(piece, k).start()

    def one_sent(piece):
        for k in range(2):

            @pl.when(jnp.logical_not(one_is_own(k)))
            def _():
                one_copy(piece, k).wait_send()

    def two_copy(piece, k):
        if k < 2:
            rows, target = aligned(col * 256, 256), nears[k]
        elif k == 2:
            rows, target = aligned(near_cols[0] * 256, 128), nears[1]
        else:
            rows, target = aligned(near_cols[1] * 256 + 128, 128), nears[0]
        view = piece_view(piece, core, rows)
        return remote(view, view, two_send.at[piece, k], two_recv.at[piece, k], target)

    def sib_copy(piece, k):
        which = col if k == 0 else near_cols[k - 1]
        view = piece_view(piece, core, aligned(which * 256, 256))
        return remote(view, view, sib_send.at[piece, k], sib_recv.at[piece, k], sib)

    def spread(piece):
        for c0 in range(2):
            rows = aligned((2 * col + c0) * 128, 128)
            pltpu.make_async_copy(
                piece_source(piece), piece_view(piece, core, rows), one_recv.at[piece, c0]
            ).wait()
        for k in range(2):
            two_copy(piece, k).start()
        sib_copy(piece, 0).start()

    def relay(piece):
        for k in range(2):
            two_copy(piece, k).wait_recv()
            two_copy(piece, k + 2).start()
            sib_copy(piece, k + 1).start()

    def relay_last(piece):
        for k in range(2, 4):
            two_copy(piece, k).wait_recv()
        sib_copy(piece, 3).start()

    def ready(piece):
        for k in range(4):
            sib_copy(piece, k).wait_recv()

    def sent(piece):
        for k in range(4):
            two_copy(piece, k).wait_send()
            sib_copy(piece, k).wait_send()

    swap_in(info_in, info, 0)
    one_start(0)
    swap_in(tok_in, tok_buf, 1)
    one_start(1)
    for i in range(2):
        load_copy(4 + i).wait()

        def round_rows(step, carry):
            rows = aligned(i * 128 + step * CHUNK, CHUNK)
            send_b[rows, :] = acc_b[rows, :].astype(jnp.bfloat16)
            return carry

        lax.fori_loop(0, 128 // CHUNK, round_rows, 0)
    swap_wait(info_in, info, 0)

    seg_first = (2 * core + par) * TOK
    seg_mine = info[0:1, aligned(seg_first, TOK)]
    flags = jnp.zeros_like(seg_mine)
    for item in range(4):
        flags = flags + jnp.where(seg_mine == item, info[2:3, item : item + 1], 0)

    def as_column(row):
        row = row.astype(jnp.float32)
        return jnp.transpose(jnp.broadcast_to(row, (128, row.shape[1])))

    cols[0] = as_column(info[1:2, 0:TOK])
    cols[1] = as_column(flags)
    seg_col[...] = as_column(info[0:1, aligned(core * 512, 512)])
    seg_row = info[0:1, :].astype(jnp.float32)
    odd = lax.rem(lax.broadcasted_iota(jnp.int32, (1, width), 1), 2)

    def encode(step, carry):
        rows = aligned(step * CHUNK, CHUNK)
        angle = cols[0, rows, 0:1] * freq_in[0:1, :]
        x_embed[rows, :] = cols[1, rows, 0:1] * sin_cos(angle, odd)
        return carry

    lax.fori_loop(0, TOK // CHUNK, encode, 0)

    def norm_first(step, carry):
        rows = aligned(step * CHUNK, CHUNK)
        value = x_embed[rows, :] + tok_buf[rows, :].astype(jnp.float32)
        x_embed[rows, :] = value
        unit, _ = normalized(value)
        row = aligned(par * TOK + step * CHUNK, CHUNK)
        h_one[row, :] = (unit * norm_in[0:1, :] + norm_in[1:2, :]).astype(jnp.bfloat16)
        return carry

    def pair_copy(buf, index):
        return remote(buf.at[own, :], buf.at[own, :], act_send.at[index], act_recv.at[index], pair)

    def embed_cells():
        swap_wait(tok_in, tok_buf, 1)
        lax.fori_loop(0, TOK // CHUNK, norm_first, 0)
        pair_copy(h_one, 3).start()

    @pl.when(home)
    def _():
        swap_in(cot_in, g_all.at[own, :], 2)
        embed_cells()
        swap_wait(cot_in, g_all.at[own, :], 2)
        pair_copy(g_all, 4).start()

    spread(0)
    relay(0)
    relay_last(0)
    spread(1)
    pl.when(jnp.logical_not(home))(embed_cells)
    one_start(2)
    ready(0)

    def project(first):
        rows = aligned(first * TOK, TOK)
        where = aligned(core * 512 + first * TOK, TOK)

        def step(i, carry):
            h = lax.div(i, 3)
            m = lax.rem(i, 3)
            out = contract(h_one[rows, :], attn_w[h, m], 1, 0) * scale_d
            qkv[m, h, where, :] = out.astype(jnp.bfloat16)
            return carry

        lax.fori_loop(0, 6, step, 0)

    def kv_copy(first, index):
        view = qkv.at[1:3, :, aligned(core * 512 + first * TOK, TOK), :]
        return remote(view, view, act_send.at[index], act_recv.at[index], sib)

    project(par)
    kv_copy(par, 5).start()
    relay(1)
    pair_copy(h_one, 3).wait_recv()
    one_start(3)
    project(flip(par))
    kv_copy(flip(par), 6).start()
    relay_last(1)
    kv_copy(par, 5).wait_recv()
    kv_copy(flip(par), 6).wait_recv()
    spread(2)

    lane_half = lax.broadcasted_iota(jnp.int32, (TOK, 128), 1)
    lane_masks = (lane_half < HD, lane_half >= HD)

    def attend(first, jj):
        rows = aligned(first * TOK, TOK)
        q_rows = aligned(core * 512 + first * TOK, TOK)
        h = lax.div(jj, 2)
        lanes = aligned(lax.rem(jj, 2) * 128, 128)
        queries = qkv[0, h, q_rows, lanes] * jnp.bfloat16(score_scale)
        keys = qkv[1, h, :, lanes]
        vals = qkv[2, h, :, lanes]
        allowed = seg_col[rows, 0:1] == seg_row
        outs = []
        for a in range(2):
            query = jnp.where(lane_masks[a], queries, jnp.bfloat16(0))
            scores = jnp.where(allowed, contract(query, keys, 1, 1), masked_score)
            top = jnp.max(scores, axis=1, keepdims=True)
            weight = jnp.exp(scores - top)
            total = jnp.sum(weight, axis=1, keepdims=True)
            share = (weight * (1.0 / total)).astype(jnp.bfloat16)
            prob[2 * jj + a, rows, :] = share
            outs.append(contract(share, vals, 1, 0))
        att[h, rows, lanes] = jnp.where(lane_masks[0], outs[0], outs[1]).astype(jnp.bfloat16)

    def attend_rows(first):
        def step(jj, carry):
            attend(first, jj)
            return carry

        lax.fori_loop(0, 4, step, 0)

    attend_rows(flip(par))

    @pl.when(jnp.logical_not(home))
    def _():
        swap_in(cot_in, g_all.at[own, :], 2)

    ready(1)

    def product_fill(product, scale, send_buf):
        def step(n, carry):
            lanes = aligned(n * WIDE, WIDE)
            send_buf[:, lanes] = (product(other, n) * scale).astype(jnp.bfloat16)
            return carry

        lax.fori_loop(0, width // WIDE, step, 0)

    def product_send(product, scale, send_buf, recv_buf, index):
        product_fill(product, scale, send_buf)
        remote(send_buf, recv_buf, act_send.at[index], act_recv.at[index], pair).start()

    def product_keep(product, scale, acc):
        def step(n, carry):
            lanes = aligned(n * WIDE, WIDE)
            acc[:, lanes] = product(own, n) * scale
            return carry

        lax.fori_loop(0, width // WIDE, step, 0)

    def split_wait(send_buf, recv_buf, index):
        remote(send_buf, recv_buf, act_send.at[index], act_recv.at[index], pair).wait()

    def out_product(rows, n):
        outs = aligned(n * WIDE, WIDE)
        total = contract(att[0, rows, :], attn_w[0, 3, outs, :], 1, 1)
        return total + contract(att[1, rows, :], attn_w[1, 3, outs, :], 1, 1)

    product_send(out_product, out_scale, send_a, recv_a, 7)
    relay(2)
    attend_rows(par)
    relay_last(2)
    spread(3)
    product_keep(out_product, out_scale, acc_a)
    split_wait(send_a, recv_a, 7)

    def norm_second(step, carry):
        rows = aligned(step * CHUNK, CHUNK)
        value = x_embed[rows, :] + (acc_a[rows, :] + recv_a[rows, :].astype(jnp.float32))
        x_mid[rows, :] = value
        unit, _ = normalized(value)
        row = aligned(par * TOK + step * CHUNK, CHUNK)
        h_two[row, :] = (unit * norm_in[2:3, :] + norm_in[3:4, :]).astype(jnp.bfloat16)
        return carry

    lax.fori_loop(0, TOK // CHUNK, norm_second, 0)
    pair_copy(h_two, 8).start()

    @pl.when(jnp.logical_not(home))
    def _():
        swap_wait(cot_in, g_all.at[own, :], 2)
        pair_copy(g_all, 4).start()

    ready(2)

    def feed_up(first):
        rows = aligned(first * TOK, TOK)

        def step(i, carry):
            h = lax.div(i, 2)
            lanes = aligned(lax.rem(i, 2) * 512, 512)
            hidden = contract(h_two[rows, :], ffn_w[h, 0, :, lanes], 1, 0) * scale_d
            gate = 0.5 + 0.5 * lax.erf(hidden * np.float32(np.sqrt(0.5)))
            act[h, rows, lanes] = (hidden * gate).astype(jnp.bfloat16)
            bell = jnp.exp(-0.5 * hidden * hidden) * np.float32(1.0 / np.sqrt(2.0 * np.pi))
            d_hid[h, rows, lanes] = (gate + hidden * bell).astype(jnp.bfloat16)
            return carry

        lax.fori_loop(0, 4, step, 0)

    def feed_back(first):
        rows = aligned(first * TOK, TOK)

        def step(i, carry):
            h = lax.div(i, 2)
            lanes = aligned(lax.rem(i, 2) * 512, 512)
            d_act = contract(g_all[rows, :], ffn_w[h, 1, :, lanes], 1, 0) * scale_f
            slope = d_hid[h, rows, lanes].astype(jnp.float32)
            d_hid[h, rows, lanes] = (d_act * slope).astype(jnp.bfloat16)
            return carry

        lax.fori_loop(0, 4, step, 0)

    def hid_product(rows, n):
        outs = aligned(n * WIDE, WIDE)
        total = contract(d_hid[0, rows, :], ffn_w[0, 0, outs, :], 1, 1)
        return total + contract(d_hid[1, rows, :], ffn_w[1, 0, outs, :], 1, 1)

    def down_product(rows, n):
        outs = aligned(n * WIDE, WIDE)
        total = contract(act[0, rows, :], ffn_w[0, 1, outs, :], 1, 1)
        return total + contract(act[1, rows, :], ffn_w[1, 1, outs, :], 1, 1)

    def grad_tile(kind, m, h, tile):
        cells = aligned(tile * 256, 256)
        if kind == 0:
            left = h_one[:, cells] if m < 3 else d_mid_all[:, cells]
            right = d_qkv[m, h] if m < 3 else att[h]
            return contract(left, right, 0, 0) * (scale_d if m < 3 else out_scale)
        left = h_two[:, cells] if m == 0 else g_all[:, cells]
        right = d_hid[h] if m == 0 else act[h]
        return contract(left, right, 0, 0) * (scale_d if m == 0 else scale_f)

    def stage_view(kind, m, rows):
        return stage.at[rows, pl.ds(m * 256, 256)] if kind == 0 else stage.at[rows, :]

    def sum_view(kind, m, rows):
        return attn_sum.at[m, rows, :] if kind == 0 else ffn_sum.at[m, rows, :]

    def slot(kind, m):
        return m if kind == 0 else 4 + m

    def tile_copy(kind, m, tile):
        rows = aligned(tile * 256, 256)
        index = slot(kind, m)
        return remote(
            stage_view(kind, m, rows),
            sum_view(kind, m, rows),
            grad_sib_send.at[index, tile],
            grad_sib_recv.at[index, tile],
            sib,
        )

    def grads_sibling(kind, m):
        def step(tile, carry):
            rows = aligned(tile * 256, 256)
            view = stage_view(kind, m, rows)
            view[...] = grad_tile(kind, m, flip(core), tile).astype(jnp.bfloat16)
            tile_copy(kind, m, tile).start()
            return carry

        lax.fori_loop(0, 4, step, 0)

    def tile_place(k):
        to_x = 1 - lax.div(k, 2)
        to_y = 1 - lax.rem(k, 2)
        x_new = x_bit + to_x - 2 * x_bit * to_x
        y_new = y_bit + to_y - 2 * y_bit * to_y
        return 2 * y_new + x_new

    def box_rows(k):
        place = (near_cols[2], near_cols[2], near_cols[0], near_cols[1], near_cols[0], near_cols[1])[k]
        return aligned(place * 256 + (0, 1, 0, 1, 1, 0)[k] * 128, 128)

    def box_view(kind, m, k):
        return attn_box.at[k, m] if kind == 0 else ffn_box.at[k, m]

    def box_copy(kind, m, k):
        index = slot(kind, m)
        return remote(
            sum_view(kind, m, box_rows(k)),
            box_view(kind, m, k),
            grad_box_send.at[index, k],
            grad_box_recv.at[index, k],
            nears[k % 2],
        )

    def stage_sent(kind, m):
        for tile in range(4):
            tile_copy(kind, m, tile).wait_send()

    def grads_own(kind, m):
        def tile(k):
            place = tile_place(k)
            total = grad_tile(kind, m, core, place)
            tile_copy(kind, m, place).wait_recv()
            view = sum_view(kind, m, aligned(place * 256, 256))
            view[...] = (total + view[...].astype(jnp.float32)).astype(jnp.bfloat16)

        def step(k, carry):
            tile(k)

            @pl.when(k == 0)
            def _():
                box_copy(kind, m, 0).start()
                box_copy(kind, m, 1).start()

            @pl.when(k == 1)
            def _():
                box_copy(kind, m, 2).start()

            @pl.when(k == 2)
            def _():
                box_copy(kind, m, 3).start()

            return carry

        lax.fori_loop(0, 4, step, 0)

    def grads_mid(kind, m):
        for k, came in ((4, 1), (5, 0)):
            box_copy(kind, m, came).wait_recv()
            view = sum_view(kind, m, box_rows(k))
            box = box_view(kind, m, came)
            view[...] = (view[...].astype(jnp.float32) + box[...].astype(jnp.float32)).astype(jnp.bfloat16)
            box_copy(kind, m, k).start()

    def own_copy(kind, m, c0):
        rows = aligned(col * 256 + c0 * 128, 128)
        dst = attn_parts.at[half, m] if kind == 0 else ffn_parts.at[half, m]
        index = slot(kind, m)
        return remote(
            sum_view(kind, m, rows),
            dst,
            grad_own_send.at[index, c0],
            grad_own_recv.at[index, half],
            (d - core + c0, quarter),
        )

    def own_is_here(c0):
        return jnp.logical_and(core == c0, t == quarter)

    def grads_columns(kind, m):
        for c0, came in ((0, (2, 5)), (1, (3, 4))):
            for k in came:
                box_copy(kind, m, k).wait_recv()
            view = sum_view(kind, m, aligned(col * 256 + c0 * 128, 128))
            total = view[...].astype(jnp.float32)
            for k in came:
                total = total + box_view(kind, m, k)[...].astype(jnp.float32)
            view[...] = total.astype(jnp.bfloat16)
        for c0 in range(2):

            @pl.when(own_is_here(c0))
            def _():
                rows = aligned(col * 256 + c0 * 128, 128)
                dst = attn_parts.at[half, m] if kind == 0 else ffn_parts.at[half, m]
                pltpu.make_async_copy(
                    sum_view(kind, m, rows), dst, grad_own_recv.at[slot(kind, m), half]
                ).start()

            @pl.when(jnp.logical_not(own_is_here(c0)))
            def _():
                own_copy(kind, m, c0).start()

    def grads_finish(kind, m):
        index = slot(kind, m)
        for k in range(2):
            src = sum_view(kind, m, aligned(col * 256, 128))
            dst = attn_parts.at[k, m] if kind == 0 else ffn_parts.at[k, m]
            pltpu.make_async_copy(src, dst, grad_own_recv.at[index, k]).wait()
        for k in range(6):
            box_copy(kind, m, k).wait_send()
        for c0 in range(2):

            @pl.when(jnp.logical_not(own_is_here(c0)))
            def _():
                own_copy(kind, m, c0).wait_send()

    feed_up(par)
    relay(3)
    pair_copy(h_two, 8).wait_recv()
    feed_up(flip(par))
    relay_last(3)
    pair_copy(g_all, 4).wait_recv()
    grads_sibling(1, 1)
    ready(3)
    feed_back(flip(par))
    product_send(hid_product, scale_d, send_a, recv_a, 9)
    feed_back(par)
    grads_own(1, 1)
    stage_sent(1, 1)
    grads_sibling(1, 0)
    product_keep(hid_product, scale_d, acc_a)
    grads_mid(1, 1)
    grads_own(1, 0)
    for piece in range(4):
        one_sent(piece)
        sent(piece)
    product_fill(down_product, scale_f, send_b)

    split_wait(send_a, recv_a, 9)

    def back_norm(step, base, gain, add, acc, out):
        rows = aligned(step * CHUNK, CHUNK)
        unit, spread_row = normalized(base[rows, :])
        d_rows = acc[rows, :] + recv_a[rows, :].astype(jnp.float32)
        scaled = d_rows * gain
        inner = jnp.mean(scaled * unit, axis=-1, keepdims=True)
        result = add + spread_row * (scaled - jnp.mean(scaled, axis=-1, keepdims=True) - unit * inner)
        out(rows, result)
        return fold_rows(d_rows * unit), fold_rows(d_rows)

    def back_second(step, carry):
        def out(rows, result):
            d_mid[rows, :] = result
            row = aligned(par * TOK + step * CHUNK, CHUNK)
            d_mid_all[row, :] = result.astype(jnp.bfloat16)

        row = aligned(par * TOK + step * CHUNK, CHUNK)
        add = g_all[row, :].astype(jnp.float32)
        d_gain, d_bias = back_norm(step, x_mid, norm_in[2:3, :], add, acc_a, out)
        norm_acc[2] = norm_acc[2] + d_gain
        norm_acc[3] = norm_acc[3] + d_bias
        return carry

    norm_acc[...] = jnp.zeros_like(norm_acc)
    lax.fori_loop(0, TOK // CHUNK, back_second, 0)
    pair_copy(d_mid_all, 11).start()
    product_keep(down_product, scale_f, acc_b)

    def back_out(first):
        rows = aligned(first * TOK, TOK)

        def step(h, carry):
            out = contract(d_mid_all[rows, :], attn_w[h, 3], 1, 0) * out_scale
            d_att[h, rows, :] = out.astype(jnp.bfloat16)
            return carry

        lax.fori_loop(0, 2, step, 0)

    def attend_back(first, last, jj):
        h = lax.div(jj, 2)
        lanes = aligned(lax.rem(jj, 2) * 128, 128)
        kept = aligned(jj * 128, 128)
        keys = qkv[1, h, :, lanes]
        vals = qkv[2, h, :, lanes]
        rows = aligned(first * TOK, TOK)
        q_rows = aligned(core * 512 + first * TOK, TOK)
        queries = qkv[0, h, q_rows, lanes] * jnp.bfloat16(score_scale)
        d_outs = d_att[h, rows, lanes]
        inner = d_outs.astype(jnp.float32) * att[h, rows, lanes].astype(jnp.float32)
        dqs = []
        dk_total = None
        dv_total = None
        for a in range(2):
            share = prob[2 * jj + a, rows, :]
            d_out = jnp.where(lane_masks[a], d_outs, jnp.bfloat16(0))
            query = jnp.where(lane_masks[a], queries, jnp.bfloat16(0))
            row_sum = jnp.sum(jnp.where(lane_masks[a], inner, 0.0), axis=1, keepdims=True)
            d_prob = contract(d_out, vals, 1, 1)
            d_score = (share.astype(jnp.float32) * (d_prob - row_sum)).astype(jnp.bfloat16)
            dqs.append(contract(d_score, keys, 1, 0))
            dk = contract(query, d_score, 0, 0)
            dv = contract(d_out, share, 0, 0)
            dk_total = dk if dk_total is None else dk_total + dk
            dv_total = dv if dv_total is None else dv_total + dv
        d_query = jnp.where(lane_masks[0], dqs[0], dqs[1]) * score_scale
        d_qkv[0, h, rows, lanes] = d_query.astype(jnp.bfloat16)
        if not last:
            ffn_w[1, 0, kept, :] = dk_total.astype(jnp.bfloat16)
            ffn_w[1, 1, kept, :] = dv_total.astype(jnp.bfloat16)
            return
        dk_tmp[...] = dk_total + ffn_w[1, 0, kept, :].astype(jnp.float32)
        dv_tmp[...] = dv_total + ffn_w[1, 1, kept, :].astype(jnp.float32)
        mine = aligned(core * 512, 512)
        theirs = aligned(flip(core) * 512, 512)
        d_qkv[1, h, :, lanes] = jnp.transpose(dk_tmp[:, mine]).astype(jnp.bfloat16)
        d_qkv[2, h, :, lanes] = jnp.transpose(dv_tmp[:, mine]).astype(jnp.bfloat16)
        kv_send[jj, 0] = jnp.transpose(dk_tmp[:, theirs]).astype(jnp.bfloat16)
        kv_send[jj, 1] = jnp.transpose(dv_tmp[:, theirs]).astype(jnp.bfloat16)
        kv_grad_copy(jj).start()

    def attend_back_rows(first, last):
        def step(jj, carry):
            attend_back(first, last, jj)
            return carry

        lax.fori_loop(0, 4, step, 0)

    def kv_grad_copy(jj):
        return remote(kv_send.at[jj], kv_recv.at[jj], act_send.at[13 + jj], act_recv.at[13 + jj], sib)

    back_out(par)
    grads_columns(1, 1)
    grads_mid(1, 0)
    attend_back_rows(par, False)
    pair_copy(d_mid_all, 11).wait_recv()
    remote(send_b, recv_b, act_send.at[10], act_recv.at[10], pair).start()
    back_out(flip(par))
    attend_back_rows(flip(par), True)
    grads_columns(1, 0)
    stage_sent(1, 0)
    grads_sibling(0, 3)

    def join_kv(jj, carry):
        kv_grad_copy(jj).wait()
        h = lax.div(jj, 2)
        lanes = aligned(lax.rem(jj, 2) * 128, 128)
        for m in range(2):
            total = d_qkv[m + 1, h, :, lanes].astype(jnp.float32) + kv_recv[jj, m].astype(jnp.float32)
            d_qkv[m + 1, h, :, lanes] = total.astype(jnp.bfloat16)
        return carry

    lax.fori_loop(0, 4, join_kv, 0)

    def first_product(rows, n):
        outs = slice(None) if n is None else aligned(n * WIDE, WIDE)
        total = None
        for h in range(2):
            for m in range(3):
                part = contract(d_qkv[m, h, rows, :], attn_w[h, m, outs, :], 1, 1)
                total = part if total is None else total + part
        return total

    def first_copy(i):
        rows = pl.ds(i * 128, 128)
        return remote(
            send_a.at[rows, :], recv_a.at[rows, :], act_send.at[19 + i], act_recv.at[19 + i], pair
        )

    for i in range(2):
        part = first_product(aligned(flip(par) * TOK + i * 128, 128), None) * scale_d
        send_a[i * 128 : (i + 1) * 128, :] = part.astype(jnp.bfloat16)
        first_copy(i).start()

    for m in range(3):
        grads_sibling(0, m)
    product_keep(first_product, scale_d, acc_a)
    grads_own(0, 3)
    for m in range(3):
        grads_own(0, m)

    split_wait(send_b, recv_b, 10)

    def finish_out(step, carry):
        rows = aligned(step * CHUNK, CHUNK)
        total = x_mid[rows, :] + (acc_b[rows, :] + recv_b[rows, :].astype(jnp.float32))
        tok_buf[rows, :] = total.astype(jnp.bfloat16)
        return carry

    lax.fori_loop(0, TOK // CHUNK, finish_out, 0)
    swap_in(tok_buf, tok_out, 12)


    for m in (3, 0, 1):
        grads_mid(0, m)
    def back_first(step, carry):
        def out(rows, result):
            send_b[rows, :] = result.astype(jnp.bfloat16)

        add = d_mid[aligned(step * CHUNK, CHUNK), :]
        d_gain, d_bias = back_norm(step, x_embed, norm_in[0:1, :], add, acc_a, out)
        norm_acc[0] = norm_acc[0] + d_gain
        norm_acc[1] = norm_acc[1] + d_bias
        return carry

    def grad_copy(i):
        rows = pl.ds(i * 128, 128)
        return send_b.at[rows, :], grad_out.at[rows, :], 17 + i

    for i in range(2):
        first_copy(i).wait()
        lax.fori_loop(4 * i, 4 * i + 4, back_first, 0)
        swap_in(*grad_copy(i))

    for row in range(4):
        norm_out[row : row + 1, :] = jnp.sum(norm_acc[row], axis=0, keepdims=True)
    norm_out[4:8, :] = jnp.zeros((4, width), jnp.float32)
    mine = 4 * core + t
    norm_recv[mine] = norm_out[...]

    def norm_copy(i):
        return remote(
            norm_out, norm_recv.at[mine], norm_send_sem.at[i], norm_recv_sem.at[mine], peers[3 + i]
        )

    def norm_far_copy(i):
        return remote(
            norm_out, norm_recv.at[8 + col], norm_send_sem.at[7 + i], norm_recv_sem.at[8 + col], nears[i]
        )

    for i in range(7):
        norm_copy(i).start()
    grads_mid(0, 2)
    grads_columns(0, 3)
    for i in range(7):
        norm_copy(i).wait_send()
    for place in range(8):

        @pl.when(place != mine)
        def _():
            pltpu.make_async_copy(norm_out, norm_recv.at[place], norm_recv_sem.at[place]).wait()

    total = norm_recv[0]
    for place in range(1, 8):
        total = total + norm_recv[place]
    norm_out[...] = total
    norm_recv[8 + col] = total
    for i in range(3):
        norm_far_copy(i).start()
    for m in range(3):
        grads_columns(0, m)
    for i in range(3):
        norm_far_copy(i).wait_send()
    for place in range(4):

        @pl.when(place != col)
        def _():
            pltpu.make_async_copy(norm_out, norm_recv.at[8 + place], norm_recv_sem.at[8 + place]).wait()

    total = norm_recv[8]
    for place in range(1, 4):
        total = total + norm_recv[8 + place]
    norm_out[...] = total
    for m in range(4):
        stage_sent(0, m)
    for m in range(2):
        grads_finish(1, m)
    for m in (3, 0, 1, 2):
        grads_finish(0, m)
    swap_sent(tok_buf, tok_out, 12)
    swap_wait(tok_buf, tok_out, 12)
    for i in range(2):
        swap_sent(*grad_copy(i))
        swap_wait(*grad_copy(i))
    swap_sent(info_in, info, 0)
    swap_sent(tok_in, tok_buf, 1)
    swap_sent(cot_in, g_all.at[own, :], 2)
    pair_copy(h_one, 3).wait_send()
    pair_copy(g_all, 4).wait_send()
    pair_copy(h_two, 8).wait_send()
    pair_copy(d_mid_all, 11).wait_send()
    kv_copy(par, 5).wait_send()
    kv_copy(flip(par), 6).wait_send()


def run_block(tok, cot, pos, seg, flag, attn_weight, ffn_weight, norm_weight, freqs):
    bf16, f32 = jnp.bfloat16, jnp.float32
    vmem, sem = pltpu.VMEM, pltpu.SemaphoreType.DMA
    width = tok.shape[1]
    wide, ff_q, head_q = 2 * TOK, ffn_weight.shape[2], attn_weight.shape[2]
    group = seg.shape[1]
    hbm = pl.BlockSpec(memory_space=pl.ANY)
    on_chip = pl.BlockSpec(memory_space=pltpu.VMEM)
    return pl.pallas_call(
        block_kernel,
        out_shape=(
            jax.ShapeDtypeStruct(tok.shape, bf16),
            jax.ShapeDtypeStruct(tok.shape, bf16),
            jax.ShapeDtypeStruct((2,) + attn_weight.shape, bf16),
            jax.ShapeDtypeStruct((2,) + ffn_weight.shape, bf16),
            jax.ShapeDtypeStruct((8, width), f32),
        ),
        in_specs=[hbm, hbm, on_chip, on_chip, on_chip, hbm, hbm, on_chip, on_chip],
        out_specs=(hbm, hbm, hbm, hbm, on_chip),
        scratch_shapes=[
            vmem((8, group), jnp.int32),
            vmem((TOK, width), bf16),
            vmem((wide, width), bf16),
            vmem((2, TOK, 128), f32),
            vmem((wide, 128), f32),
            vmem((TOK, width), f32),
            vmem((TOK, width), f32),
            vmem((TOK, width), f32),
            vmem((wide, width), bf16),
            vmem((wide, width), bf16),
            vmem((wide, width), bf16),
            vmem((2, 4, width, head_q), bf16),
            vmem((2, 2, width, ff_q), bf16),
            vmem((3, 2, group, head_q), bf16),
            vmem((8, wide, group), bf16),
            vmem((2, wide, head_q), bf16),
            vmem((2, wide, head_q), bf16),
            vmem((2, wide, ff_q), bf16),
            vmem((2, wide, ff_q), bf16),
            vmem((TOK, width), bf16),
            vmem((TOK, width), bf16),
            vmem((TOK, width), bf16),
            vmem((TOK, width), bf16),
            vmem((TOK, width), f32),
            vmem((TOK, width), f32),
            vmem((3, 2, wide, head_q), bf16),
            vmem((4, 2, wide, 128), bf16),
            vmem((4, 2, wide, 128), bf16),
            vmem((128, group), f32),
            vmem((128, group), f32),
            vmem((2, width, ff_q), bf16),
            vmem((width, ff_q), bf16),
            vmem((4, width, head_q), bf16),
            vmem((6, 2, 128, ff_q), bf16),
            vmem((6, 4, 128, head_q), bf16),
            vmem((4, 8, width), f32),
            vmem((12, 8, width), f32),
            sem((4, 2)),
            sem((4, 2)),
            sem((4, 4)),
            sem((4, 4)),
            sem((4, 4)),
            sem((4, 4)),
            sem((21,)),
            sem((21,)),
            sem((6, 4)),
            sem((6, 4)),
            sem((6, 6)),
            sem((6, 6)),
            sem((6, 2)),
            sem((6, 2)),
            sem((10,)),
            sem((12,)),
            vmem(attn_weight.shape, bf16),
            sem((6,)),
            vmem((8, group), jnp.int32),
        ],
        compiler_params=pltpu.CompilerParams(
            collective_id=0, has_side_effects=True, vmem_limit_bytes=VMEM_LIMIT
        ),
        cost_estimate=pl.CostEstimate(
            flops=30_000_000_000, bytes_accessed=30_000_000, transcendentals=10_000_000
        ),
        name="block",
    )(tok, cot, pos, seg, flag, attn_weight, ffn_weight, norm_weight, freqs)


VMEM_LIMIT = 63 * 2**20


def adam_kernel(grad_scale, *refs):
    (
        out_in,
        dx_in,
        attn_parts,
        ffn_parts,
        norm_rows,
        attn_w,
        attn_m,
        attn_e,
        ffn_w,
        ffn_m,
        ffn_e,
        norm_w,
        norm_m,
        norm_e,
        out_out,
        dx_out,
        attn_g,
        ffn_g,
        norm_g,
    ) = refs[:19]
    news = refs[19:]

    def update(weight, moments, ema, grad, new_refs):
        new_weight, new_moments, new_ema = adam_update(weight[...], moments[...], ema[...], grad * grad_scale)
        new_refs[0][...] = new_weight
        new_refs[1][...] = new_moments
        new_refs[2][...] = new_ema

    out_out[...] = out_in[...]
    dx_out[...] = dx_in[...]
    attn_g[...] = attn_parts[0].astype(jnp.float32) + attn_parts[1].astype(jnp.float32)
    ffn_g[...] = ffn_parts[0].astype(jnp.float32) + ffn_parts[1].astype(jnp.float32)
    norm_g[...] = norm_rows[0:4, :]
    update(attn_w, attn_m, attn_e, attn_g[...], news[0:3])
    update(ffn_w, ffn_m, ffn_e, ffn_g[...], news[3:6])
    update(norm_w, norm_m, norm_e, norm_g[...], news[6:9])


def run_adam(grad_scale, steps, out_tokens, grad_tokens, attn_parts, ffn_parts, norm_rows, *states):
    def cut(array, dim):
        shape = tuple(n // steps if i == dim else n for i, n in enumerate(array.shape))
        return pl.BlockSpec(shape, lambda i: tuple(i if n == dim else 0 for n in range(len(shape))))

    def same(array):
        return pl.BlockSpec(array.shape, lambda i: (0,) * array.ndim)

    attn, ffn, norm = states[0:3], states[3:6], states[6:9]
    state_specs = [cut(a, a.ndim - 2) for a in attn + ffn] + [same(a) for a in norm]
    in_specs = [cut(out_tokens, 0), cut(grad_tokens, 0), cut(attn_parts, 2), cut(ffn_parts, 2), same(norm_rows)]
    heads = [out_tokens, grad_tokens, attn[0], ffn[0], norm[0]]
    head_specs = [cut(out_tokens, 0), cut(grad_tokens, 0), cut(attn[0], 1), cut(ffn[0], 1), same(norm[0])]
    return pl.pallas_call(
        lambda *refs: adam_kernel(grad_scale, *refs),
        grid=(steps,),
        out_shape=tuple(jax.ShapeDtypeStruct(a.shape, a.dtype) for a in heads + list(states)),
        in_specs=in_specs + state_specs,
        out_specs=tuple(head_specs + state_specs),
        compiler_params=pltpu.CompilerParams(vmem_limit_bytes=VMEM_LIMIT),
        cost_estimate=pl.CostEstimate(flops=8_000_000, bytes_accessed=16_000_000, transcendentals=800_000),
        name="adam",
    )(out_tokens, grad_tokens, attn_parts, ffn_parts, norm_rows, *states)


def local_fast(
    tokens,
    cotangent,
    positions,
    segment_ids,
    spatial_flag,
    attn_weight,
    attn_moments,
    attn_ema,
    ffn_weight,
    ffn_moments,
    ffn_ema,
    norm_weight,
    norm_moments,
    norm_ema,
):
    width = tokens.shape[1]
    group = segment_ids.shape[1]
    exponent = -2.0 * (np.arange(width) // 2) / width
    freqs = jnp.asarray(np.tile((10000.0**exponent).astype(np.float32), (8, 1)))
    grad_scale = float(group * lax.axis_size("dp")) ** (-0.5)
    out_tokens, grad_tokens, attn_parts, ffn_parts, norm_rows = run_block(
        tokens,
        cotangent,
        positions,
        segment_ids,
        spatial_flag,
        attn_weight,
        ffn_weight,
        norm_weight,
        freqs,
    )
    return run_adam(
        grad_scale,
        4,
        out_tokens,
        grad_tokens,
        attn_parts,
        ffn_parts,
        norm_rows,
        attn_weight,
        attn_moments,
        attn_ema,
        ffn_weight,
        ffn_moments,
        ffn_ema,
        norm_weight,
        norm_moments,
        norm_ema,
    )


def solution(mesh):
    placed = (
        P(("dp", "tensor"), None),
        P(("dp", "tensor"), None),
        P("dp", "tensor"),
        P("dp", None),
        P("dp", None),
        P(None, "dp", "tensor"),
        P(None, None, "dp", "tensor"),
        P(None, "dp", "tensor"),
        P(None, "dp", "tensor"),
        P(None, None, "dp", "tensor"),
        P(None, "dp", "tensor"),
        P(),
        P(),
        P(),
    )
    fast = mesh.shape["dp"] == 8 and mesh.shape["tensor"] == 4
    return jax.shard_map(
        local_fast if fast else local,
        mesh=mesh,
        in_specs=placed,
        out_specs=(
            P(("dp", "tensor"), None),
            P(("dp", "tensor"), None),
            P(None, "dp", "tensor"),
            P(None, "dp", "tensor"),
            P(),
            P(None, "dp", "tensor"),
            P(None, None, "dp", "tensor"),
            P(None, "dp", "tensor"),
            P(None, "dp", "tensor"),
            P(None, None, "dp", "tensor"),
            P(None, "dp", "tensor"),
            P(),
            P(),
            P(),
        ),
        check_vma=False,
    )
```

```python
import jax
import jax.numpy as jnp
import numpy as np
from jax import lax
from jax.experimental import pallas as pl
from jax.experimental.pallas import tpu as pltpu
from jax.sharding import PartitionSpec as P

HD = 64
FF = 4096
STEP = 5


out_gain = 16.0
beta_one = 0.6
beta_two = 0.95
adam_eps = 1e-08
decay_rate = 0.1
learn_value = 0.25
ema_value = 0.7
norm_eps = 1e-05
masked_score = -1e30


def sinusoid(cell_pos, model_width):
    feature = jnp.arange(model_width, dtype=jnp.int32)
    freqs = jnp.power(10000.0, -(2 * (feature // 2)).astype(jnp.float32) / model_width)
    angles = cell_pos.astype(jnp.float32)[:, None] * freqs[None, :]
    return jnp.where(feature % 2 == 0, jnp.sin(angles), jnp.cos(angles))


def layer_norm(inputs, gain_vec, bias_vec):
    row_mean = jnp.mean(inputs, axis=-1, keepdims=True)
    centred = inputs - row_mean
    row_var = jnp.mean(centred * centred, axis=-1, keepdims=True)
    return centred * lax.rsqrt(row_var + norm_eps) * gain_vec + bias_vec


def exact_gelu(values):
    return jax.nn.gelu(values, approximate=False)


def adam_update(weight, moments, ema_weight, gradient):
    step_num = float(STEP)
    first_mom = beta_one * moments[0] + (1.0 - beta_one) * gradient
    second_mom = beta_two * moments[1] + (1.0 - beta_two) * gradient * gradient
    fix_one = 1.0 - beta_one**step_num
    fix_two = 1.0 - beta_two**step_num
    update = first_mom / fix_one / (jnp.sqrt(second_mom / fix_two) + adam_eps) + decay_rate * weight
    new_weight = weight - learn_value * update
    new_ema = ema_value * ema_weight + (1.0 - ema_value) * new_weight
    return (new_weight, jnp.stack([first_mom, second_mom]), new_ema)


def dot_last(left, right):
    return lax.dot_general(
        left, right, (((1,), (1,)), ((), ())), preferred_element_type=jnp.float32
    )


def dot_first(left, right):
    return lax.dot_general(
        left, right, (((0,), (0,)), ((), ())), preferred_element_type=jnp.float32
    )


def local(
    tokens,
    cotangent,
    positions,
    segment_ids,
    spatial_flag,
    attn_weight,
    attn_moments,
    attn_ema,
    ffn_weight,
    ffn_moments,
    ffn_ema,
    norm_weight,
    norm_moments,
    norm_ema,
):
    tok_rows = tokens.shape[0]
    model_width = tokens.shape[1]
    seg_all = segment_ids[0]
    group_len = seg_all.shape[0]
    q_block = min(512, group_len)
    block_count = group_len // q_block
    scale_d = model_width ** (-0.5)
    scale_f = FF ** (-0.5)
    score_scale = HD ** (-0.5)
    out_scale = out_gain * scale_d
    grad_scale = float(group_len * lax.axis_size("dp")) ** (-0.5)
    row_first = lax.axis_index("tensor") * tok_rows
    seg_own = lax.dynamic_slice_in_dim(seg_all, row_first, tok_rows, 0)
    item_ids = jnp.arange(spatial_flag.shape[1], dtype=jnp.int32)
    cell_flag = jnp.sum(
        jnp.where(seg_own[:, None] == item_ids[None, :], spatial_flag[0][None, :], 0), axis=1
    )
    x_embed = tokens.astype(jnp.float32) + cell_flag.astype(jnp.float32)[:, None] * sinusoid(
        positions[0], model_width
    )
    attn_half, ffn_half = (
        lax.all_gather(attn_weight.astype(jnp.bfloat16), "dp", axis=1, tiled=True),
        lax.all_gather(ffn_weight.astype(jnp.bfloat16), "dp", axis=1, tiled=True),
    )
    head_width = attn_half.shape[2]
    head_count = head_width // HD
    h_one_f, norm_one_pull = jax.vjp(layer_norm, x_embed, norm_weight[0], norm_weight[1])
    h_one = lax.all_gather(h_one_f.astype(jnp.bfloat16), "tensor", axis=0, tiled=True)
    projected = (
        jnp.einsum("gd,cdj->cgj", h_one, attn_half[:3], preferred_element_type=jnp.float32)
        * scale_d
    ).astype(jnp.bfloat16)
    queries = projected[0].reshape(group_len, head_count, HD)
    key_rows = projected[1].reshape(group_len, head_count, HD)
    val_rows = projected[2].reshape(group_len, head_count, HD)

    def score_block(block_index):
        row_start = block_index * q_block
        query_blk = lax.dynamic_slice_in_dim(queries, row_start, q_block, 0)
        seg_blk = lax.dynamic_slice_in_dim(seg_all, row_start, q_block, 0)
        scores = (
            jnp.einsum("qhd,khd->hqk", query_blk, key_rows, preferred_element_type=jnp.float32)
            * score_scale
        )
        allowed = (seg_blk[:, None] == seg_all[None, :])[None]
        return (query_blk, jnp.where(allowed, scores, masked_score), allowed)

    def attend(block_index):
        query_blk, scores, allowed = score_block(block_index)
        row_top = jnp.max(scores, axis=2, keepdims=True)
        exp_rows = jnp.exp(scores - row_top)
        row_total = jnp.sum(exp_rows, axis=2, keepdims=True)
        prob_rows = (exp_rows / row_total).astype(jnp.bfloat16)
        result = jnp.einsum("hqk,khd->qhd", prob_rows, val_rows, preferred_element_type=jnp.float32)
        return (result, (row_top + jnp.log(row_total))[:, :, 0])

    attended, log_totals = lax.map(attend, jnp.arange(block_count))
    attended = attended.reshape(group_len, head_width).astype(jnp.bfloat16)
    branch = lax.psum_scatter(
        dot_last(attended, attn_half[3]) * out_scale, "tensor", scatter_dimension=0, tiled=True
    )
    x_mid = x_embed + branch
    h_two_f, norm_two_pull = jax.vjp(layer_norm, x_mid, norm_weight[2], norm_weight[3])
    h_two = lax.all_gather(h_two_f.astype(jnp.bfloat16), "tensor", axis=0, tiled=True)
    hidden = jnp.dot(h_two, ffn_half[0], preferred_element_type=jnp.float32) * scale_d
    activated_f, gelu_pull = jax.vjp(exact_gelu, hidden)
    activated = activated_f.astype(jnp.bfloat16)
    ffn_out = lax.psum_scatter(
        dot_last(activated, ffn_half[1]) * scale_f, "tensor", scatter_dimension=0, tiled=True
    )
    out_tokens = (x_mid + ffn_out).astype(jnp.bfloat16)
    dy_own = cotangent.astype(jnp.float32)
    dy_all = lax.all_gather(cotangent, "tensor", axis=0, tiled=True)
    d_act = jnp.dot(dy_all, ffn_half[1], preferred_element_type=jnp.float32) * scale_f
    d_hidden = gelu_pull(d_act)[0].astype(jnp.bfloat16)
    grad_down = dot_first(dy_all, activated) * scale_f
    grad_up = dot_first(h_two, d_hidden) * scale_d
    d_h_two = lax.psum_scatter(
        dot_last(d_hidden, ffn_half[0]) * scale_d, "tensor", scatter_dimension=0, tiled=True
    )
    d_mid_part, d_gain_two, d_bias_two = norm_two_pull(d_h_two)
    d_mid = dy_own + d_mid_part
    d_mid_all = lax.all_gather(d_mid.astype(jnp.bfloat16), "tensor", axis=0, tiled=True)
    d_att = (
        jnp.dot(d_mid_all, attn_half[3], preferred_element_type=jnp.float32) * out_scale
    ).astype(jnp.bfloat16)
    grad_mix = dot_first(d_mid_all, attended) * out_scale
    d_att3 = d_att.reshape(group_len, head_count, HD)

    def attend_back(state_pair, block_index):
        dk_sum, dv_sum = state_pair
        query_blk, scores, allowed = score_block(block_index)
        row_start = block_index * q_block
        dout_blk = lax.dynamic_slice_in_dim(d_att3, row_start, q_block, 0)
        prob_rows = jnp.where(allowed, jnp.exp(scores - log_totals[block_index][:, :, None]), 0.0)
        dv_sum = dv_sum + jnp.einsum(
            "hqk,qhd->khd",
            prob_rows.astype(jnp.bfloat16),
            dout_blk,
            preferred_element_type=jnp.float32,
        )
        d_prob = jnp.einsum("qhd,khd->hqk", dout_blk, val_rows, preferred_element_type=jnp.float32)
        d_score = (
            prob_rows * (d_prob - jnp.sum(d_prob * prob_rows, axis=2, keepdims=True))
        ).astype(jnp.bfloat16)
        dq_blk = (
            jnp.einsum("hqk,khd->qhd", d_score, key_rows, preferred_element_type=jnp.float32)
            * score_scale
        )
        dk_sum = (
            dk_sum
            + jnp.einsum("hqk,qhd->khd", d_score, query_blk, preferred_element_type=jnp.float32)
            * score_scale
        )
        return ((dk_sum, dv_sum), dq_blk)

    zero_keys = jnp.zeros((group_len, head_count, HD), jnp.float32)
    (dk_sum, dv_sum), dq_blocks = lax.scan(
        attend_back, (zero_keys, zero_keys), jnp.arange(block_count)
    )
    d_proj = jnp.stack(
        [
            dq_blocks.reshape(group_len, head_width),
            dk_sum.reshape(group_len, head_width),
            dv_sum.reshape(group_len, head_width),
        ]
    ).astype(jnp.bfloat16)
    grad_proj = (
        jnp.einsum("gd,cgj->cdj", h_one, d_proj, preferred_element_type=jnp.float32) * scale_d
    )
    d_h_one = lax.psum_scatter(
        jnp.einsum("cgj,cdj->gd", d_proj, attn_half[:3], preferred_element_type=jnp.float32)
        * scale_d,
        "tensor",
        scatter_dimension=0,
        tiled=True,
    )
    d_embed_part, d_gain_one, d_bias_one = norm_one_pull(d_h_one)
    grad_tokens = (d_mid + d_embed_part).astype(jnp.bfloat16)
    attn_part = jnp.concatenate([grad_proj, grad_mix[None]], axis=0)
    ffn_part = jnp.stack([grad_up, grad_down])
    attn_grad, ffn_grad = (
        lax.psum_scatter(attn_part, "dp", scatter_dimension=1, tiled=True),
        lax.psum_scatter(ffn_part, "dp", scatter_dimension=1, tiled=True),
    )
    norm_grad = lax.psum(
        jnp.stack([d_gain_one, d_bias_one, d_gain_two, d_bias_two]), ("dp", "tensor")
    )
    attn_new, attn_mom_new, attn_ema_new = adam_update(
        attn_weight, attn_moments, attn_ema, attn_grad * grad_scale
    )
    ffn_new, ffn_mom_new, ffn_ema_new = adam_update(
        ffn_weight, ffn_moments, ffn_ema, ffn_grad * grad_scale
    )
    norm_new, norm_mom_new, norm_ema_new = adam_update(
        norm_weight, norm_moments, norm_ema, norm_grad * grad_scale
    )
    return (
        out_tokens,
        grad_tokens,
        attn_grad,
        ffn_grad,
        norm_grad,
        attn_new,
        attn_mom_new,
        attn_ema_new,
        ffn_new,
        ffn_mom_new,
        ffn_ema_new,
        norm_new,
        norm_mom_new,
        norm_ema_new,
    )


MESH = pl.DeviceIdType.MESH
TOK = 256
WIDE = 512
CHUNK = 32
PIECES = ("qkv", "out", "up", "down")


def contract(left, right, left_dim, right_dim):
    return lax.dot_general(
        left,
        right,
        (((left_dim,), (right_dim,)), ((), ())),
        preferred_element_type=jnp.float32,
    )


def flip(bit):
    return 1 - bit


def aligned(start, size):
    return pl.ds(pl.multiple_of(start, size), size)


def sin_cos(angle, odd):
    turns = jnp.floor(angle * (2.0 / np.pi) + 0.5)
    rest = angle - turns * 1.5703125
    rest = rest - turns * 4.837512969970703125e-4
    rest = rest - turns * 7.54978995489188216e-8
    quadrant = turns.astype(jnp.int32) + odd
    square = rest * rest
    sine = ((-1.9515295891e-4 * square + 8.3321608736e-3) * square - 1.6666654611e-1) * square
    sine = sine * rest + rest
    cosine = (2.443315711809948e-5 * square - 1.388731625493765e-3) * square
    cosine = (cosine + 4.166664568298827e-2) * square * square - 0.5 * square + 1.0
    value = jnp.where((quadrant & 1) == 1, cosine, sine)
    return jnp.where((quadrant & 2) == 2, -value, value)


def gelu_gate(hidden, bell):
    step = 1.0 / (1.0 + np.float32(0.3275911 * np.sqrt(0.5)) * jnp.abs(hidden))
    tail = np.float32(0.5 * 1.061405429) * step - np.float32(0.5 * 1.453152027)
    tail = tail * step + np.float32(0.5 * 1.421413741)
    tail = tail * step - np.float32(0.5 * 0.284496736)
    tail = (tail * step + np.float32(0.5 * 0.254829592)) * step * bell
    return jnp.where(hidden < 0.0, tail, 1.0 - tail)


def normalized(rows):
    centred = rows - jnp.mean(rows, axis=-1, keepdims=True)
    spread = lax.rsqrt(jnp.mean(centred * centred, axis=-1, keepdims=True) + norm_eps)
    return centred * spread, spread


def fold_rows(values):
    total = values[0:8]
    for first in range(8, values.shape[0], 8):
        total = total + values[first : first + 8]
    return total


def block_kernel(
    tok_in,
    cot_in,
    pos_in,
    seg_in,
    flag_in,
    attn_in,
    ffn_in,
    norm_in,
    freq_in,
    tok_out,
    grad_out,
    attn_parts,
    ffn_parts,
    norm_out,
    info,
    tok_buf,
    g_all,
    cols,
    seg_col,
    x_embed,
    x_mid,
    d_mid,
    h_one,
    h_two,
    d_mid_all,
    attn_w,
    ffn_w,
    qkv,
    prob,
    att,
    d_att,
    act,
    d_hid,
    send_a,
    send_b,
    recv_a,
    recv_b,
    acc_a,
    acc_b,
    d_qkv,
    kv_send,
    kv_recv,
    dk_tmp,
    dv_tmp,
    ffn_sum,
    stage,
    attn_sum,
    ffn_box,
    attn_box,
    norm_acc,
    norm_recv,
    one_send,
    one_recv,
    two_send,
    two_recv,
    sib_send,
    sib_recv,
    act_send,
    act_recv,
    grad_sib_send,
    grad_sib_recv,
    grad_box_send,
    grad_box_recv,
    grad_own_send,
    grad_own_recv,
    norm_send_sem,
    norm_recv_sem,
    attn_half,
    load_sem,
    info_in,
):
    width = freq_in.shape[1]
    scale_d = width ** (-0.5)
    scale_f = FF ** (-0.5)
    out_scale = out_gain * scale_d
    score_scale = HD ** (-0.5)

    d = lax.axis_index("dp")
    t = lax.axis_index("tensor")
    core = lax.rem(d, 2)
    col = lax.div(d, 2)
    x_bit = lax.rem(col, 2)
    y_bit = lax.div(col, 2)
    par = lax.rem(t, 2)
    half = lax.div(t, 2)
    quarter = 2 * par + core
    home = core == half
    d_sib = d + 1 - 2 * core
    d_x = d + 2 - 4 * x_bit
    d_y = d + 4 - 8 * y_bit
    d_xy = d_x + 4 - 8 * y_bit
    t_pair = t + 1 - 2 * par
    t_far = t + 2 - 4 * half
    sib = (d_sib, t)
    pair = (d, t_pair)
    swap = (d_sib, t_far)
    nears = ((d_x, t), (d_y, t), (d_xy, t))
    near_cols = (lax.div(d_x, 2), lax.div(d_y, 2), lax.div(d_xy, 2))

    def remote(src, dst, send, recv, device):
        return pltpu.make_async_remote_copy(
            src_ref=src, dst_ref=dst, send_sem=send, recv_sem=recv, device_id=device, device_id_type=MESH
        )

    def load_copy(i):
        if i < 4:
            src, dst = attn_in.at[i], acc_a.at[0:128, pl.ds(i * 256, 256)]
        else:
            src, dst = ffn_in.at[i - 4], acc_b.at[pl.ds((i - 4) * 128, 128), :]
        return pltpu.make_async_copy(src, dst, load_sem.at[i])

    for i in range(6):
        load_copy(i).start()
    info_in[...] = jnp.zeros_like(info_in)
    info_in[0:1, :] = seg_in[...]
    info_in[1:2, 0:TOK] = pos_in[...]
    info_in[2:3, 0 : flag_in.shape[1]] = flag_in[...]

    barrier = pltpu.get_barrier_semaphore()
    peers = list(nears)
    for dd in (d, d_sib):
        for tt in (t, t_pair, t_far, t_pair + t_far - t):
            peers.append((dd, tt))
    peers = peers[:3] + peers[4:]
    for peer in peers:
        pl.semaphore_signal(barrier, inc=1, device_id=peer, device_id_type=MESH)
    for i in range(4):
        load_copy(i).wait()
        attn_half[i] = acc_a[0:128, i * 256 : (i + 1) * 256].astype(jnp.bfloat16)
    pl.semaphore_wait(barrier, len(peers))

    own = aligned(par * TOK, TOK)
    other = aligned(flip(par) * TOK, TOK)

    def swap_in(src, dst, index):
        @pl.when(home)
        def _():
            pltpu.make_async_copy(src, dst, act_recv.at[index]).start()

        @pl.when(jnp.logical_not(home))
        def _():
            remote(src, dst, act_send.at[index], act_recv.at[index], swap).start()

    def swap_wait(src, dst, index):
        pltpu.make_async_copy(src, dst, act_recv.at[index]).wait()

    def swap_sent(src, dst, index):
        @pl.when(jnp.logical_not(home))
        def _():
            remote(src, dst, act_send.at[index], act_recv.at[index], swap).wait_send()

    def piece_view(piece, h, rows):
        if piece == 0:
            return attn_w.at[h, 0:3, rows, :]
        if piece == 1:
            return attn_w.at[h, 3, rows, :]
        return ffn_w.at[h, piece - 2, rows, :]

    def piece_source(piece):
        if piece == 0:
            return attn_half.at[0:3]
        if piece == 1:
            return attn_half.at[3]
        return send_b.at[pl.ds((piece - 2) * 128, 128), :]

    def one_copy(piece, k):
        dst = piece_view(piece, par, aligned(d * 128, 128))
        target = (d - core + par, half + 2 * k)
        return remote(
            piece_source(piece), dst, one_send.at[piece, k], one_recv.at[piece, core], target
        )

    def one_is_own(k):
        if k == 0:
            return jnp.logical_and(core == par, t == half)
        return jnp.logical_and(core == par, t == half + 2)

    def one_start(piece):
        for k in range(2):

            @pl.when(one_is_own(k))
            def _():
                dst = piece_view(piece, par, aligned(d * 128, 128))
                pltpu.make_async_copy(piece_source(piece), dst, one_recv.at[piece, core]).start()

            @pl.when(jnp.logical_not(one_is_own(k)))
            def _():
                one_copy(piece, k).start()

    def one_sent(piece):
        for k in range(2):

            @pl.when(jnp.logical_not(one_is_own(k)))
            def _():
                one_copy(piece, k).wait_send()

    def two_copy(piece, k):
        which = (col, col, col, col, near_cols[0], near_cols[1])[k]
        rows = aligned(which * 256 + (0, 1, 1, 0, 0, 1)[k] * 128, 128)
        view = piece_view(piece, core, rows)
        target = nears[(0, 1, 0, 1, 1, 0)[k]]
        return remote(view, view, two_send.at[piece, k], two_recv.at[piece, k], target)

    def sib_copy(piece, k):
        which = col if k == 0 else near_cols[k - 1]
        view = piece_view(piece, core, aligned(which * 256, 256))
        return remote(view, view, sib_send.at[piece, k], sib_recv.at[piece, k], sib)

    def spread(piece):
        for c0 in range(2):
            rows = aligned((2 * col + c0) * 128, 128)
            pltpu.make_async_copy(
                piece_source(piece), piece_view(piece, core, rows), one_recv.at[piece, c0]
            ).wait()
        for k in range(4):
            two_copy(piece, k).start()
        sib_copy(piece, 0).start()

    def relay(piece):
        for k in range(2):
            two_copy(piece, k).wait_recv()
            two_copy(piece, k + 4).start()

    def relay_last(piece):
        for k in range(2):
            two_copy(piece, k + 2).wait_recv()
            sib_copy(piece, k + 1).start()
        for k in range(4, 6):
            two_copy(piece, k).wait_recv()
        sib_copy(piece, 3).start()

    def ready(piece):
        for k in range(4):
            sib_copy(piece, k).wait_recv()

    def sent(piece):
        for k in range(6):
            two_copy(piece, k).wait_send()
        for k in range(4):
            sib_copy(piece, k).wait_send()

    swap_in(info_in, info, 0)
    one_start(0)
    swap_in(tok_in, tok_buf, 1)
    one_start(1)
    for i in range(2):
        load_copy(4 + i).wait()

        def round_rows(step, carry):
            rows = aligned(i * 128 + step * CHUNK, CHUNK)
            send_b[rows, :] = acc_b[rows, :].astype(jnp.bfloat16)
            return carry

        lax.fori_loop(0, 128 // CHUNK, round_rows, 0)
    swap_wait(info_in, info, 0)

    seg_first = (2 * core + par) * TOK
    seg_mine = info[0:1, aligned(seg_first, TOK)]
    flags = jnp.zeros_like(seg_mine)
    for item in range(4):
        flags = flags + jnp.where(seg_mine == item, info[2:3, item : item + 1], 0)

    def as_column(row):
        row = row.astype(jnp.float32)
        return jnp.transpose(jnp.broadcast_to(row, (128, row.shape[1])))

    cols[0] = as_column(info[1:2, 0:TOK])
    cols[1] = as_column(flags)
    seg_col[...] = as_column(info[0:1, aligned(core * 512, 512)])
    seg_row = info[0:1, :].astype(jnp.float32)
    odd = lax.rem(lax.broadcasted_iota(jnp.int32, (1, width), 1), 2)

    def encode(step, carry):
        rows = aligned(step * CHUNK, CHUNK)
        angle = cols[0, rows, 0:1] * freq_in[0:1, :]
        x_embed[rows, :] = cols[1, rows, 0:1] * sin_cos(angle, odd)
        return carry

    lax.fori_loop(0, TOK // CHUNK, encode, 0)

    def norm_first(step, carry):
        rows = aligned(step * CHUNK, CHUNK)
        value = x_embed[rows, :] + tok_buf[rows, :].astype(jnp.float32)
        x_embed[rows, :] = value
        unit, _ = normalized(value)
        row = aligned(par * TOK + step * CHUNK, CHUNK)
        h_one[row, :] = (unit * norm_in[0:1, :] + norm_in[1:2, :]).astype(jnp.bfloat16)
        return carry

    def pair_copy(buf, index):
        return remote(buf.at[own, :], buf.at[own, :], act_send.at[index], act_recv.at[index], pair)

    def embed_cells():
        swap_wait(tok_in, tok_buf, 1)
        lax.fori_loop(0, TOK // CHUNK, norm_first, 0)
        pair_copy(h_one, 3).start()

    @pl.when(home)
    def _():
        swap_in(cot_in, g_all.at[own, :], 2)
        embed_cells()
        swap_wait(cot_in, g_all.at[own, :], 2)
        pair_copy(g_all, 4).start()

    spread(0)
    relay(0)
    spread(1)
    relay_last(0)
    pl.when(jnp.logical_not(home))(embed_cells)
    one_start(2)
    ready(0)

    def project(first):
        rows = aligned(first * TOK, TOK)
        where = aligned(core * 512 + first * TOK, TOK)

        def step(i, carry):
            h = lax.div(i, 3)
            m = lax.rem(i, 3)
            out = contract(h_one[rows, :], attn_w[h, m], 1, 0) * scale_d
            qkv[m, h, where, :] = out.astype(jnp.bfloat16)
            return carry

        lax.fori_loop(0, 6, step, 0)

    def kv_copy(first, index):
        view = qkv.at[1:3, :, aligned(core * 512 + first * TOK, TOK), :]
        return remote(view, view, act_send.at[index], act_recv.at[index], sib)

    project(par)
    kv_copy(par, 5).start()
    relay(1)
    pair_copy(h_one, 3).wait_recv()
    one_start(3)
    project(flip(par))
    kv_copy(flip(par), 6).start()
    relay_last(1)
    spread(2)
    kv_copy(par, 5).wait_recv()
    kv_copy(flip(par), 6).wait_recv()

    lane_half = lax.broadcasted_iota(jnp.int32, (TOK, 128), 1)
    lane_masks = (lane_half < HD, lane_half >= HD)

    def attend(first, jj):
        rows = aligned(first * TOK, TOK)
        q_rows = aligned(core * 512 + first * TOK, TOK)
        h = lax.div(jj, 2)
        lanes = aligned(lax.rem(jj, 2) * 128, 128)
        queries = qkv[0, h, q_rows, lanes] * jnp.bfloat16(score_scale)
        keys = qkv[1, h, :, lanes]
        vals = qkv[2, h, :, lanes]
        allowed = seg_col[rows, 0:1] == seg_row
        outs = []
        for a in range(2):
            query = jnp.where(lane_masks[a], queries, jnp.bfloat16(0))
            scores = jnp.where(allowed, contract(query, keys, 1, 1), masked_score)
            top = jnp.max(scores, axis=1, keepdims=True)
            weight = jnp.exp(scores - top)
            total = jnp.sum(weight, axis=1, keepdims=True)
            share = (weight * (1.0 / total)).astype(jnp.bfloat16)
            prob[2 * jj + a, rows, :] = share
            outs.append(contract(share, vals, 1, 0))
        att[h, rows, lanes] = jnp.where(lane_masks[0], outs[0], outs[1]).astype(jnp.bfloat16)

    def attend_rows(first):
        def step(jj, carry):
            attend(first, jj)
            return carry

        lax.fori_loop(0, 4, step, 0)

    attend_rows(flip(par))

    @pl.when(jnp.logical_not(home))
    def _():
        swap_in(cot_in, g_all.at[own, :], 2)

    ready(1)

    def product_fill(product, scale, send_buf):
        def step(n, carry):
            lanes = aligned(n * WIDE, WIDE)
            send_buf[:, lanes] = (product(other, n) * scale).astype(jnp.bfloat16)
            return carry

        lax.fori_loop(0, width // WIDE, step, 0)

    def half_copy(i, index):
        rows = pl.ds(i * 128, 128)
        return remote(
            send_a.at[rows, :], recv_a.at[rows, :], act_send.at[index + i], act_recv.at[index + i], pair
        )

    def product_halves(product, scale, index):
        for i in range(2):
            part = product(aligned(flip(par) * TOK + i * 128, 128), None) * scale
            send_a[i * 128 : (i + 1) * 128, :] = part.astype(jnp.bfloat16)
            half_copy(i, index).start()

    def pair_half(buf, i, index):
        rows = aligned(par * TOK + i * 128, 128)
        view = buf.at[rows, :]
        return remote(view, view, act_send.at[index + i], act_recv.at[index + i], pair)

    def product_keep(product, scale, acc):
        def step(n, carry):
            lanes = aligned(n * WIDE, WIDE)
            acc[:, lanes] = product(own, n) * scale
            return carry

        lax.fori_loop(0, width // WIDE, step, 0)

    def split_wait(send_buf, recv_buf, index):
        remote(send_buf, recv_buf, act_send.at[index], act_recv.at[index], pair).wait()

    def out_product(rows, n):
        outs = slice(None) if n is None else aligned(n * WIDE, WIDE)
        total = contract(att[0, rows, :], attn_w[0, 3, outs, :], 1, 1)
        return total + contract(att[1, rows, :], attn_w[1, 3, outs, :], 1, 1)

    product_halves(out_product, out_scale, 21)
    relay(2)
    attend_rows(par)
    relay_last(2)
    spread(3)
    product_keep(out_product, out_scale, acc_a)

    def norm_second(step, carry):
        rows = aligned(step * CHUNK, CHUNK)
        value = x_embed[rows, :] + (acc_a[rows, :] + recv_a[rows, :].astype(jnp.float32))
        x_mid[rows, :] = value
        unit, _ = normalized(value)
        row = aligned(par * TOK + step * CHUNK, CHUNK)
        h_two[row, :] = (unit * norm_in[2:3, :] + norm_in[3:4, :]).astype(jnp.bfloat16)
        return carry

    for i in range(2):
        half_copy(i, 21).wait()
        lax.fori_loop(4 * i, 4 * i + 4, norm_second, 0)
        pair_half(h_two, i, 23).start()

    @pl.when(jnp.logical_not(home))
    def _():
        swap_wait(cot_in, g_all.at[own, :], 2)
        pair_copy(g_all, 4).start()

    ready(2)

    def feed_up(first):
        rows = aligned(first * TOK, TOK)

        def step(i, carry):
            h = lax.div(i, 2)
            lanes = aligned(lax.rem(i, 2) * 512, 512)
            hidden = contract(h_two[rows, :], ffn_w[h, 0, :, lanes], 1, 0) * scale_d
            bell = jnp.exp(-0.5 * hidden * hidden)
            gate = gelu_gate(hidden, bell)
            act[h, rows, lanes] = (hidden * gate).astype(jnp.bfloat16)
            slope = gate + hidden * bell * np.float32(1.0 / np.sqrt(2.0 * np.pi))
            d_hid[h, rows, lanes] = slope.astype(jnp.bfloat16)
            return carry

        lax.fori_loop(0, 4, step, 0)

    def feed_back(first):
        rows = aligned(first * TOK, TOK)

        def step(i, carry):
            h = lax.div(i, 2)
            lanes = aligned(lax.rem(i, 2) * 512, 512)
            d_act = contract(g_all[rows, :], ffn_w[h, 1, :, lanes], 1, 0) * scale_f
            slope = d_hid[h, rows, lanes].astype(jnp.float32)
            d_hid[h, rows, lanes] = (d_act * slope).astype(jnp.bfloat16)
            return carry

        lax.fori_loop(0, 4, step, 0)

    def hid_product(rows, n):
        outs = slice(None) if n is None else aligned(n * WIDE, WIDE)
        total = contract(d_hid[0, rows, :], ffn_w[0, 0, outs, :], 1, 1)
        return total + contract(d_hid[1, rows, :], ffn_w[1, 0, outs, :], 1, 1)

    def down_product(rows, n):
        outs = aligned(n * WIDE, WIDE)
        total = contract(act[0, rows, :], ffn_w[0, 1, outs, :], 1, 1)
        return total + contract(act[1, rows, :], ffn_w[1, 1, outs, :], 1, 1)

    def grad_product(matrix, h, n):
        if matrix < 3:
            return contract(h_one[...], d_qkv[matrix, h], 0, 0) * scale_d
        if matrix == 3:
            return contract(d_mid_all[...], att[h], 0, 0) * out_scale
        lanes = aligned(n * 256, 256)
        if matrix == 4:
            return contract(h_two[...], d_hid[h, :, lanes], 0, 0) * scale_d
        return contract(g_all[...], act[h, :, lanes], 0, 0) * scale_f

    def tiles(matrix):
        return 1 if matrix < 4 else 4

    def stage_view(matrix, n):
        return stage.at[:, aligned((matrix if matrix < 4 else n) * 256, 256)]

    def tile_view(matrix, n):
        return attn_sum.at[matrix] if matrix < 4 else ffn_sum.at[matrix - 4, :, aligned(n * 256, 256)]

    def tile_copy(matrix, n):
        return remote(
            stage_view(matrix, n),
            tile_view(matrix, n),
            grad_sib_send.at[matrix, n],
            grad_sib_recv.at[matrix, n],
            sib,
        )

    def grads_sibling(matrix):
        def step(n, carry):
            view = stage_view(matrix, n)
            view[...] = grad_product(matrix, flip(core), n).astype(jnp.bfloat16)
            tile_copy(matrix, n).start()
            return carry

        if tiles(matrix) == 1:
            step(0, 0)
        else:
            lax.fori_loop(0, tiles(matrix), step, 0)

    def stage_sent(matrix):
        for n in range(tiles(matrix)):
            tile_copy(matrix, n).wait_send()

    def grads_own(matrix):
        def step(n, carry):
            total = grad_product(matrix, core, n)
            tile_copy(matrix, n).wait_recv()
            view = tile_view(matrix, n)
            view[...] = (total + view[...].astype(jnp.float32)).astype(jnp.bfloat16)
            return carry

        if tiles(matrix) == 1:
            step(0, 0)
        else:
            lax.fori_loop(0, tiles(matrix), step, 0)

    def sum_view(group, rows):
        if group == 0:
            return attn_sum.at[0:3, rows, :]
        return attn_sum.at[3, rows, :] if group == 1 else ffn_sum.at[group - 2, rows, :]

    def box_rows(k):
        place = (near_cols[2], near_cols[2], near_cols[0], near_cols[1], near_cols[0], near_cols[1])[k]
        return aligned(place * 256 + (0, 1, 0, 1, 1, 0)[k] * 128, 128)

    def box_view(group, k):
        if group == 0:
            return attn_box.at[k, 0:3]
        return attn_box.at[k, 3] if group == 1 else ffn_box.at[k, group - 2]

    def box_copy(group, k):
        return remote(
            sum_view(group, box_rows(k)),
            box_view(group, k),
            grad_box_send.at[group, k],
            grad_box_recv.at[group, k],
            nears[k % 2],
        )

    def grads_start(group):
        for k in range(4):
            box_copy(group, k).start()

    def grads_mid(group):
        for k, came in ((4, 1), (5, 0)):
            box_copy(group, came).wait_recv()
            view = sum_view(group, box_rows(k))
            box = box_view(group, came)
            view[...] = (view[...].astype(jnp.float32) + box[...].astype(jnp.float32)).astype(jnp.bfloat16)
            box_copy(group, k).start()

    def part_view(group, k):
        if group == 0:
            return attn_parts.at[k, 0:3]
        return attn_parts.at[k, 3] if group == 1 else ffn_parts.at[k, group - 2]

    def own_rows(c0):
        return aligned(col * 256 + c0 * 128, 128)

    def own_copy(group, c0):
        return remote(
            sum_view(group, own_rows(c0)),
            part_view(group, half),
            grad_own_send.at[group, c0],
            grad_own_recv.at[group, half],
            (d - core + c0, quarter),
        )

    def own_is_here(c0):
        return jnp.logical_and(core == c0, t == quarter)

    def grads_columns(group):
        for c0, came in ((0, (2, 5)), (1, (3, 4))):
            for k in came:
                box_copy(group, k).wait_recv()
            view = sum_view(group, own_rows(c0))
            total = view[...].astype(jnp.float32)
            for k in came:
                total = total + box_view(group, k)[...].astype(jnp.float32)
            view[...] = total.astype(jnp.bfloat16)

            @pl.when(own_is_here(c0))
            def _():
                pltpu.make_async_copy(
                    sum_view(group, own_rows(c0)), part_view(group, half), grad_own_recv.at[group, half]
                ).start()

            @pl.when(jnp.logical_not(own_is_here(c0)))
            def _():
                own_copy(group, c0).start()

    def grads_finish(group):
        for k in range(2):
            pltpu.make_async_copy(
                sum_view(group, own_rows(0)), part_view(group, k), grad_own_recv.at[group, k]
            ).wait()
        for k in range(6):
            box_copy(group, k).wait_send()
        for c0 in range(2):

            @pl.when(jnp.logical_not(own_is_here(c0)))
            def _():
                own_copy(group, c0).wait_send()

    feed_up(par)
    relay(3)
    for i in range(2):
        pair_half(h_two, i, 23).wait_recv()
    feed_up(flip(par))
    relay_last(3)
    pair_copy(g_all, 4).wait_recv()
    grads_sibling(5)
    grads_own(5)
    grads_start(3)
    ready(3)
    feed_back(flip(par))
    product_halves(hid_product, scale_d, 25)
    feed_back(par)
    stage_sent(5)
    grads_sibling(4)
    grads_mid(3)
    grads_own(4)
    grads_start(2)
    product_keep(hid_product, scale_d, acc_a)
    for piece in range(4):
        one_sent(piece)
        sent(piece)
    product_fill(down_product, scale_f, send_b)


    def back_norm(step, base, gain, add, acc, out):
        rows = aligned(step * CHUNK, CHUNK)
        unit, spread_row = normalized(base[rows, :])
        d_rows = acc[rows, :] + recv_a[rows, :].astype(jnp.float32)
        scaled = d_rows * gain
        inner = jnp.mean(scaled * unit, axis=-1, keepdims=True)
        result = add + spread_row * (scaled - jnp.mean(scaled, axis=-1, keepdims=True) - unit * inner)
        out(rows, result)
        return fold_rows(d_rows * unit), fold_rows(d_rows)

    def back_second(step, carry):
        def out(rows, result):
            d_mid[rows, :] = result
            row = aligned(par * TOK + step * CHUNK, CHUNK)
            d_mid_all[row, :] = result.astype(jnp.bfloat16)

        row = aligned(par * TOK + step * CHUNK, CHUNK)
        add = g_all[row, :].astype(jnp.float32)
        d_gain, d_bias = back_norm(step, x_mid, norm_in[2:3, :], add, acc_a, out)
        norm_acc[2] = norm_acc[2] + d_gain
        norm_acc[3] = norm_acc[3] + d_bias
        return carry

    norm_acc[...] = jnp.zeros_like(norm_acc)
    for i in range(2):
        half_copy(i, 25).wait()
        lax.fori_loop(4 * i, 4 * i + 4, back_second, 0)
        pair_half(d_mid_all, i, 27).start()
    product_keep(down_product, scale_f, acc_b)

    def back_out(first):
        rows = aligned(first * TOK, TOK)

        def step(h, carry):
            out = contract(d_mid_all[rows, :], attn_w[h, 3], 1, 0) * out_scale
            d_att[h, rows, :] = out.astype(jnp.bfloat16)
            return carry

        lax.fori_loop(0, 2, step, 0)

    def attend_back(first, last, jj):
        h = lax.div(jj, 2)
        lanes = aligned(lax.rem(jj, 2) * 128, 128)
        kept = aligned(jj * 128, 128)
        keys = qkv[1, h, :, lanes]
        vals = qkv[2, h, :, lanes]
        rows = aligned(first * TOK, TOK)
        q_rows = aligned(core * 512 + first * TOK, TOK)
        queries = qkv[0, h, q_rows, lanes] * jnp.bfloat16(score_scale)
        d_outs = d_att[h, rows, lanes]
        inner = d_outs.astype(jnp.float32) * att[h, rows, lanes].astype(jnp.float32)
        dqs = []
        dk_total = None
        dv_total = None
        for a in range(2):
            share = prob[2 * jj + a, rows, :]
            d_out = jnp.where(lane_masks[a], d_outs, jnp.bfloat16(0))
            query = jnp.where(lane_masks[a], queries, jnp.bfloat16(0))
            row_sum = jnp.sum(jnp.where(lane_masks[a], inner, 0.0), axis=1, keepdims=True)
            d_prob = contract(d_out, vals, 1, 1)
            d_score = (share.astype(jnp.float32) * (d_prob - row_sum)).astype(jnp.bfloat16)
            dqs.append(contract(d_score, keys, 1, 0))
            dk = contract(query, d_score, 0, 0)
            dv = contract(d_out, share, 0, 0)
            dk_total = dk if dk_total is None else dk_total + dk
            dv_total = dv if dv_total is None else dv_total + dv
        d_query = jnp.where(lane_masks[0], dqs[0], dqs[1]) * score_scale
        d_qkv[0, h, rows, lanes] = d_query.astype(jnp.bfloat16)
        if not last:
            ffn_w[1, 0, kept, :] = dk_total.astype(jnp.bfloat16)
            ffn_w[1, 1, kept, :] = dv_total.astype(jnp.bfloat16)
            return
        dk_tmp[...] = dk_total + ffn_w[1, 0, kept, :].astype(jnp.float32)
        dv_tmp[...] = dv_total + ffn_w[1, 1, kept, :].astype(jnp.float32)
        mine = aligned(core * 512, 512)
        theirs = aligned(flip(core) * 512, 512)
        d_qkv[1, h, :, lanes] = jnp.transpose(dk_tmp[:, mine]).astype(jnp.bfloat16)
        d_qkv[2, h, :, lanes] = jnp.transpose(dv_tmp[:, mine]).astype(jnp.bfloat16)
        kv_send[jj, 0] = jnp.transpose(dk_tmp[:, theirs]).astype(jnp.bfloat16)
        kv_send[jj, 1] = jnp.transpose(dv_tmp[:, theirs]).astype(jnp.bfloat16)
        kv_grad_copy(jj).start()

    def attend_back_rows(first, last):
        def step(jj, carry):
            attend_back(first, last, jj)
            return carry

        lax.fori_loop(0, 4, step, 0)

    def kv_grad_copy(jj):
        return remote(kv_send.at[jj], kv_recv.at[jj], act_send.at[13 + jj], act_recv.at[13 + jj], sib)

    back_out(par)
    attend_back_rows(par, False)
    grads_columns(3)
    grads_mid(2)
    for i in range(2):
        pair_half(d_mid_all, i, 27).wait_recv()
    remote(send_b, recv_b, act_send.at[10], act_recv.at[10], pair).start()
    back_out(flip(par))
    attend_back_rows(flip(par), True)
    stage_sent(4)
    grads_sibling(3)

    def join_kv(jj, carry):
        kv_grad_copy(jj).wait()
        h = lax.div(jj, 2)
        lanes = aligned(lax.rem(jj, 2) * 128, 128)
        for m in range(2):
            total = d_qkv[m + 1, h, :, lanes].astype(jnp.float32) + kv_recv[jj, m].astype(jnp.float32)
            d_qkv[m + 1, h, :, lanes] = total.astype(jnp.bfloat16)
        return carry

    lax.fori_loop(0, 4, join_kv, 0)

    def first_product(rows, n):
        outs = slice(None) if n is None else aligned(n * WIDE, WIDE)
        total = None
        for h in range(2):
            for m in range(3):
                part = contract(d_qkv[m, h, rows, :], attn_w[h, m, outs, :], 1, 1)
                total = part if total is None else total + part
        return total

    product_halves(first_product, scale_d, 19)
    grads_columns(2)

    for matrix in range(3):
        grads_sibling(matrix)
    product_keep(first_product, scale_d, acc_a)

    grads_own(3)
    grads_start(1)
    for matrix in range(3):
        grads_own(matrix)
    grads_mid(1)
    grads_start(0)

    split_wait(send_b, recv_b, 10)

    def finish_out(step, carry):
        rows = aligned(step * CHUNK, CHUNK)
        total = x_mid[rows, :] + (acc_b[rows, :] + recv_b[rows, :].astype(jnp.float32))
        tok_buf[rows, :] = total.astype(jnp.bfloat16)
        return carry

    lax.fori_loop(0, TOK // CHUNK, finish_out, 0)
    swap_in(tok_buf, tok_out, 12)
    grads_mid(0)
    grads_columns(1)

    def back_first(step, carry):
        def out(rows, result):
            send_b[rows, :] = result.astype(jnp.bfloat16)

        add = d_mid[aligned(step * CHUNK, CHUNK), :]
        d_gain, d_bias = back_norm(step, x_embed, norm_in[0:1, :], add, acc_a, out)
        norm_acc[0] = norm_acc[0] + d_gain
        norm_acc[1] = norm_acc[1] + d_bias
        return carry

    def grad_copy(i):
        rows = pl.ds(i * 128, 128)
        return send_b.at[rows, :], grad_out.at[rows, :], 17 + i

    for i in range(2):
        half_copy(i, 19).wait()
        lax.fori_loop(4 * i, 4 * i + 4, back_first, 0)

    for row in range(4):
        norm_out[row : row + 1, :] = jnp.sum(norm_acc[row], axis=0, keepdims=True)
    norm_out[4:8, :] = jnp.zeros((4, width), jnp.float32)
    mine = 4 * core + t
    norm_recv[mine] = norm_out[...]

    def norm_copy(i):
        return remote(
            norm_out, norm_recv.at[mine], norm_send_sem.at[i], norm_recv_sem.at[mine], peers[3 + i]
        )

    def norm_far_copy(i):
        return remote(
            norm_out, norm_recv.at[8 + col], norm_send_sem.at[7 + i], norm_recv_sem.at[8 + col], nears[i]
        )

    for i in range(7):
        norm_copy(i).start()
    for i in range(2):
        swap_in(*grad_copy(i))
    grads_columns(0)
    for i in range(7):
        norm_copy(i).wait_send()
    for place in range(8):

        @pl.when(place != mine)
        def _():
            pltpu.make_async_copy(norm_out, norm_recv.at[place], norm_recv_sem.at[place]).wait()

    total = norm_recv[0]
    for place in range(1, 8):
        total = total + norm_recv[place]
    norm_out[...] = total
    norm_recv[8 + col] = total
    for i in range(3):
        norm_far_copy(i).start()
    for i in range(3):
        norm_far_copy(i).wait_send()
    for place in range(4):

        @pl.when(place != col)
        def _():
            pltpu.make_async_copy(norm_out, norm_recv.at[8 + place], norm_recv_sem.at[8 + place]).wait()

    total = norm_recv[8]
    for place in range(1, 4):
        total = total + norm_recv[8 + place]
    norm_out[...] = total
    for matrix in range(4):
        stage_sent(matrix)
    for group in (3, 2, 1, 0):
        grads_finish(group)
    swap_sent(tok_buf, tok_out, 12)
    swap_wait(tok_buf, tok_out, 12)
    for i in range(2):
        swap_sent(*grad_copy(i))
        swap_wait(*grad_copy(i))
    swap_sent(info_in, info, 0)
    swap_sent(tok_in, tok_buf, 1)
    swap_sent(cot_in, g_all.at[own, :], 2)
    pair_copy(h_one, 3).wait_send()
    pair_copy(g_all, 4).wait_send()
    for i in range(2):
        pair_half(h_two, i, 23).wait_send()
        pair_half(d_mid_all, i, 27).wait_send()
    kv_copy(par, 5).wait_send()
    kv_copy(flip(par), 6).wait_send()


def run_block(tok, cot, pos, seg, flag, attn_weight, ffn_weight, norm_weight, freqs):
    bf16, f32 = jnp.bfloat16, jnp.float32
    vmem, sem = pltpu.VMEM, pltpu.SemaphoreType.DMA
    width = tok.shape[1]
    wide, ff_q, head_q = 2 * TOK, ffn_weight.shape[2], attn_weight.shape[2]
    group = seg.shape[1]
    hbm = pl.BlockSpec(memory_space=pl.ANY)
    on_chip = pl.BlockSpec(memory_space=pltpu.VMEM)
    return pl.pallas_call(
        block_kernel,
        out_shape=(
            jax.ShapeDtypeStruct(tok.shape, bf16),
            jax.ShapeDtypeStruct(tok.shape, bf16),
            jax.ShapeDtypeStruct((2,) + attn_weight.shape, bf16),
            jax.ShapeDtypeStruct((2,) + ffn_weight.shape, bf16),
            jax.ShapeDtypeStruct((8, width), f32),
        ),
        in_specs=[hbm, hbm, on_chip, on_chip, on_chip, hbm, hbm, on_chip, on_chip],
        out_specs=(hbm, hbm, hbm, hbm, on_chip),
        scratch_shapes=[
            vmem((8, group), jnp.int32),
            vmem((TOK, width), bf16),
            vmem((wide, width), bf16),
            vmem((2, TOK, 128), f32),
            vmem((wide, 128), f32),
            vmem((TOK, width), f32),
            vmem((TOK, width), f32),
            vmem((TOK, width), f32),
            vmem((wide, width), bf16),
            vmem((wide, width), bf16),
            vmem((wide, width), bf16),
            vmem((2, 4, width, head_q), bf16),
            vmem((2, 2, width, ff_q), bf16),
            vmem((3, 2, group, head_q), bf16),
            vmem((8, wide, group), bf16),
            vmem((2, wide, head_q), bf16),
            vmem((2, wide, head_q), bf16),
            vmem((2, wide, ff_q), bf16),
            vmem((2, wide, ff_q), bf16),
            vmem((TOK, width), bf16),
            vmem((TOK, width), bf16),
            vmem((TOK, width), bf16),
            vmem((TOK, width), bf16),
            vmem((TOK, width), f32),
            vmem((TOK, width), f32),
            vmem((3, 2, wide, head_q), bf16),
            vmem((4, 2, wide, 128), bf16),
            vmem((4, 2, wide, 128), bf16),
            vmem((128, group), f32),
            vmem((128, group), f32),
            vmem((2, width, ff_q), bf16),
            vmem((width, ff_q), bf16),
            vmem((4, width, head_q), bf16),
            vmem((6, 2, 128, ff_q), bf16),
            vmem((6, 4, 128, head_q), bf16),
            vmem((4, 8, width), f32),
            vmem((12, 8, width), f32),
            sem((4, 2)),
            sem((4, 2)),
            sem((4, 6)),
            sem((4, 6)),
            sem((4, 4)),
            sem((4, 4)),
            sem((29,)),
            sem((29,)),
            sem((6, 4)),
            sem((6, 4)),
            sem((4, 6)),
            sem((4, 6)),
            sem((4, 2)),
            sem((4, 2)),
            sem((10,)),
            sem((12,)),
            vmem(attn_weight.shape, bf16),
            sem((6,)),
            vmem((8, group), jnp.int32),
        ],
        compiler_params=pltpu.CompilerParams(
            collective_id=0, has_side_effects=True, vmem_limit_bytes=VMEM_LIMIT
        ),
        cost_estimate=pl.CostEstimate(
            flops=30_000_000_000, bytes_accessed=30_000_000, transcendentals=10_000_000
        ),
        name="block",
    )(tok, cot, pos, seg, flag, attn_weight, ffn_weight, norm_weight, freqs)


VMEM_LIMIT = 63 * 2**20


def adam_kernel(grad_scale, *refs):
    (
        out_in,
        dx_in,
        attn_parts,
        ffn_parts,
        norm_rows,
        attn_w,
        attn_m,
        attn_e,
        ffn_w,
        ffn_m,
        ffn_e,
        norm_w,
        norm_m,
        norm_e,
        out_out,
        dx_out,
        attn_g,
        ffn_g,
        norm_g,
    ) = refs[:19]
    news = refs[19:]

    def update(weight, moments, ema, grad, new_refs):
        new_weight, new_moments, new_ema = adam_update(weight[...], moments[...], ema[...], grad * grad_scale)
        new_refs[0][...] = new_weight
        new_refs[1][...] = new_moments
        new_refs[2][...] = new_ema

    out_out[...] = out_in[...]
    dx_out[...] = dx_in[...]
    attn_g[...] = attn_parts[0].astype(jnp.float32) + attn_parts[1].astype(jnp.float32)
    ffn_g[...] = ffn_parts[0].astype(jnp.float32) + ffn_parts[1].astype(jnp.float32)
    norm_g[...] = norm_rows[0:4, :]
    update(attn_w, attn_m, attn_e, attn_g[...], news[0:3])
    update(ffn_w, ffn_m, ffn_e, ffn_g[...], news[3:6])
    update(norm_w, norm_m, norm_e, norm_g[...], news[6:9])


def run_adam(grad_scale, steps, out_tokens, grad_tokens, attn_parts, ffn_parts, norm_rows, *states):
    def cut(array, dim):
        shape = tuple(n // steps if i == dim else n for i, n in enumerate(array.shape))
        return pl.BlockSpec(shape, lambda i: tuple(i if n == dim else 0 for n in range(len(shape))))

    def same(array):
        return pl.BlockSpec(array.shape, lambda i: (0,) * array.ndim)

    attn, ffn, norm = states[0:3], states[3:6], states[6:9]
    state_specs = [cut(a, a.ndim - 2) for a in attn + ffn] + [same(a) for a in norm]
    in_specs = [cut(out_tokens, 0), cut(grad_tokens, 0), cut(attn_parts, 2), cut(ffn_parts, 2), same(norm_rows)]
    heads = [out_tokens, grad_tokens, attn[0], ffn[0], norm[0]]
    head_specs = [cut(out_tokens, 0), cut(grad_tokens, 0), cut(attn[0], 1), cut(ffn[0], 1), same(norm[0])]
    return pl.pallas_call(
        lambda *refs: adam_kernel(grad_scale, *refs),
        grid=(steps,),
        out_shape=tuple(jax.ShapeDtypeStruct(a.shape, a.dtype) for a in heads + list(states)),
        in_specs=in_specs + state_specs,
        out_specs=tuple(head_specs + state_specs),
        compiler_params=pltpu.CompilerParams(vmem_limit_bytes=VMEM_LIMIT),
        cost_estimate=pl.CostEstimate(flops=8_000_000, bytes_accessed=16_000_000, transcendentals=800_000),
        name="adam",
    )(out_tokens, grad_tokens, attn_parts, ffn_parts, norm_rows, *states)


def local_fast(
    tokens,
    cotangent,
    positions,
    segment_ids,
    spatial_flag,
    attn_weight,
    attn_moments,
    attn_ema,
    ffn_weight,
    ffn_moments,
    ffn_ema,
    norm_weight,
    norm_moments,
    norm_ema,
):
    width = tokens.shape[1]
    group = segment_ids.shape[1]
    exponent = -2.0 * (np.arange(width) // 2) / width
    freqs = jnp.asarray(np.tile((10000.0**exponent).astype(np.float32), (8, 1)))
    grad_scale = float(group * lax.axis_size("dp")) ** (-0.5)
    out_tokens, grad_tokens, attn_parts, ffn_parts, norm_rows = run_block(
        tokens,
        cotangent,
        positions,
        segment_ids,
        spatial_flag,
        attn_weight,
        ffn_weight,
        norm_weight,
        freqs,
    )
    return run_adam(
        grad_scale,
        2,
        out_tokens,
        grad_tokens,
        attn_parts,
        ffn_parts,
        norm_rows,
        attn_weight,
        attn_moments,
        attn_ema,
        ffn_weight,
        ffn_moments,
        ffn_ema,
        norm_weight,
        norm_moments,
        norm_ema,
    )


def solution(mesh):
    placed = (
        P(("dp", "tensor"), None),
        P(("dp", "tensor"), None),
        P("dp", "tensor"),
        P("dp", None),
        P("dp", None),
        P(None, "dp", "tensor"),
        P(None, None, "dp", "tensor"),
        P(None, "dp", "tensor"),
        P(None, "dp", "tensor"),
        P(None, None, "dp", "tensor"),
        P(None, "dp", "tensor"),
        P(),
        P(),
        P(),
    )
    fast = mesh.shape["dp"] == 8 and mesh.shape["tensor"] == 4
    return jax.shard_map(
        local_fast if fast else local,
        mesh=mesh,
        in_specs=placed,
        out_specs=(
            P(("dp", "tensor"), None),
            P(("dp", "tensor"), None),
            P(None, "dp", "tensor"),
            P(None, "dp", "tensor"),
            P(),
            P(None, "dp", "tensor"),
            P(None, None, "dp", "tensor"),
            P(None, "dp", "tensor"),
            P(None, "dp", "tensor"),
            P(None, None, "dp", "tensor"),
            P(None, "dp", "tensor"),
            P(),
            P(),
            P(),
        ),
        check_vma=False,
    )
```
